32 devices in a mesh: ctx: 8 (over z, x), sec: 2 (over y), dp: 2 (over core).
Axes of the slice: x: 2, y: 2, z: 4, core: 2. Of those that a mesh axis runs over, the one named last changes fastest.
Arguments:
- fresh_input: bfloat16 [2, 2048, 1536], P('dp', 'ctx'), may hold values from -6 to 6
- carried: bfloat16 [2, 2, 2048, 1536], P('sec', 'dp', 'ctx'), may hold values from -6 to 6
- qkv_weight: bfloat16 [2, 1536, 4608], P('sec', ('ctx', 'dp')), as said below
- out_weight: bfloat16 [2, 1536, 1536], P('sec', ('ctx', 'dp')), may hold values from -0.15625 to 0.15625
- rate_weight: bfloat16 [2, 1536, 6], P('sec', ('ctx', 'dp')), may hold values from -0.15625 to 0.15625
- fast_state: float32 [2, 2, 3, 6, 768, 256], P('sec', 'dp', None, None, 'ctx'), may hold values from -6 to 6
Outputs:
- passed: bfloat16 [2, 2, 2048, 1536], P('sec', 'dp', 'ctx')
- new_state: float32 [2, 2, 3, 6, 768, 256], P('sec', 'dp', None, None, 'ctx')
The draws below stay inside these ranges and needn't reach their ends.
Inputs may be any that keep to these rules, and one draw needn't show every extreme that they name: Every entry of qkv_weight is at most 6 / sqrt(1536) in magnitude.
All inputs are finite; a program needn't handle non-finite values.
Results may differ from the reference program's by a relative error of at most 0.022.
Values may be sent and summed in bfloat16 or wider, within the bound.
A program may use at most 128 MiB of HBM per device.

```python
import jax
import jax.numpy as jnp
from jax import lax

D = 1536
HEADS = 6
HD = 256
FH = 768
NS_STEPS = 2
GROUP = 2048
N_CTX = 8
N_SEC = 2
N_DP = 2


def draw_qkv_weight(key, part):
    columns = 3 * HEADS * HD
    entry_key, pick_key, high_key, low_key = jax.random.split(key, 4)
    entries = jax.random.truncated_normal(entry_key, -6.0, 6.0, (N_SEC, D, columns), jnp.float32)
    high_share = 0.45
    low_bottom = -1.6
    low_top = -1.1
    picked = jax.random.bernoulli(pick_key, high_share, (N_SEC, 1, columns))
    high_scale = jnp.exp(jax.random.uniform(high_key, (N_SEC, 1, columns), jnp.float32, -0.2, 0.0))
    low_scale = jnp.exp(jax.random.uniform(low_key, (N_SEC, 1, columns), jnp.float32, low_bottom, low_top))
    position = jnp.arange(columns, dtype=jnp.int32)[None, None, :]
    column_scale = jnp.where(position >= HEADS * HD, jnp.where(picked, high_scale, low_scale), 1.0)
    return (entries * column_scale * float(D) ** (-0.5)).astype(jnp.bfloat16)


def levels(rng, shape, pieces, least, top_value):
    factor_of = 1.0
    for dim, blocks in pieces:
        heights = jax.random.uniform(jax.random.fold_in(jax.random.fold_in(rng, 6), dim), (blocks,), jnp.float32, least / len(pieces), top_value / len(pieces))
        factor_of = factor_of * jnp.repeat(jnp.exp(heights), shape[dim] // blocks).reshape((-1,) + (1,) * (len(shape) - 1 - dim))
    return factor_of


def centred(own_key, dims, scale, limit, pieces=(), kind=jnp.bfloat16):
    values = jax.random.normal(own_key, dims, jnp.float32) * scale
    if len(pieces) > 0:
        values = levels(own_key, dims, pieces, -0.22, 0.18) * values
    return jnp.clip(values, min=-limit, max=limit).astype(kind)


def setup_inputs(seed: int = 0) -> dict:
    keys = jax.random.split(jax.random.key(seed), 7)
    return {
        "fresh_input": centred(keys[0], (N_DP, GROUP, D), 1.0, 6.0, ((0, 2), (1, 8))),
        "carried": centred(keys[1], (N_SEC, N_DP, GROUP, D), 1.0, 6.0, ((0, 2), (1, 2), (2, 8))),
        "qkv_weight": draw_qkv_weight(jax.random.fold_in(keys[6], 71), 0),
        "out_weight": centred(keys[3], (N_SEC, HEADS * HD, D), (HEADS * HD) ** -0.5, 0.15625, ((0, 2), (1, 16))),
        "rate_weight": centred(keys[4], (N_SEC, D, HEADS), D ** -0.5, 0.15625, ((0, 2), (1, 16))),
        "fast_state": centred(keys[5], (N_SEC, N_DP, 3, HEADS, FH, HD), 1.0, 6.0, ((0, 2), (1, 2), (4, 8)), jnp.float32),
    }


linear_coef = 3.4445
cubic_coef = -4.775
quintic_coef = 2.0315
update_scale = 8.0
highest = lax.Precision.HIGHEST

def swish(values):
    return values * jax.nn.sigmoid(values)

def unit_rows(values):
    return values / jnp.sqrt(lax.optimization_barrier(jnp.sum(values * values, axis=-1, keepdims=True)) + 1e-06)

def to_half(values):
    return lax.optimization_barrier(values.astype(jnp.bfloat16)).astype(jnp.float32)

def group_terms(key_rows, value_rows, rates, gate_fast, up_fast, down_fast):
    keys_wide = key_rows.astype(jnp.float32)
    gate_pre = jnp.einsum('thd,hfd->thf', keys_wide, gate_fast)
    up_pre = jnp.einsum('thd,hfd->thf', keys_wide, up_fast)
    sigma = jax.nn.sigmoid(gate_pre)
    gate_act = gate_pre * sigma
    key_hidden = to_half(gate_act * up_pre)
    scaled_values = to_half(rates[:, :, None] * value_rows.astype(jnp.float32))
    hidden_grad = -jnp.einsum('thd,hfd->thf', scaled_values, down_fast)
    up_grad = to_half(hidden_grad * gate_act)
    gate_grad = to_half(hidden_grad * up_pre * sigma * (1.0 + gate_pre * (1.0 - sigma)))
    grad_gate = jnp.einsum('thf,thd->hfd', gate_grad, keys_wide)
    grad_up = jnp.einsum('thf,thd->hfd', up_grad, keys_wide)
    grad_down = -jnp.einsum('thf,thd->hfd', key_hidden, scaled_values)
    return jnp.stack([grad_gate, grad_up, grad_down])

def gram_sum(current):
    blocks = current.reshape(3, HEADS, N_CTX, FH // N_CTX, HD)
    parts = jnp.einsum('mhnrd,mhnre->mhnde', blocks, blocks, precision=highest)
    return lax.optimization_barrier(jnp.sum(to_half(parts), axis=2))

def orthogonalize(gradient):
    current = gradient
    for iteration in range(NS_STEPS):
        square = gram_sum(current)
        if iteration == 0:
            inverse_norm = lax.rsqrt(jnp.trace(square, axis1=-2, axis2=-1) + 1e-06)[:, :, None, None]
            current = current * inverse_norm
            square = square * inverse_norm * inverse_norm
        product = jnp.einsum('mhrd,mhde->mhre', current, square, precision=highest)
        current = linear_coef * current + cubic_coef * product + quintic_coef * jnp.einsum('mhrd,mhde->mhre', product, square, precision=highest)
    return current

def fast_layer(inputs, qkv_weight, out_weight, rate_weight, fast_state):
    count = inputs.shape[0]
    projected = jnp.dot(inputs, qkv_weight, preferred_element_type=jnp.float32).reshape(count, 3, HEADS, HD)
    query_rows = unit_rows(swish(projected[:, 0])).astype(jnp.bfloat16)
    key_rows = unit_rows(swish(projected[:, 1])).astype(jnp.bfloat16)
    value_rows = projected[:, 2].astype(jnp.bfloat16)
    rates = jax.nn.softplus(jnp.dot(inputs, rate_weight, preferred_element_type=jnp.float32))
    fast_round = to_half(fast_state)
    gate_fast, up_fast, down_fast = (fast_round[0], fast_round[1], fast_round[2])
    query_wide = query_rows.astype(jnp.float32)
    gate_pre = jnp.einsum('thd,hfd->thf', query_wide, gate_fast)
    up_pre = jnp.einsum('thd,hfd->thf', query_wide, up_fast)
    hidden = to_half(swish(gate_pre) * up_pre)
    mixture = jnp.einsum('thf,hfd->thd', hidden, down_fast)
    head_out = (mixture * lax.rsqrt(lax.optimization_barrier(jnp.mean(mixture * mixture, axis=-1, keepdims=True)) + 1e-05)).astype(jnp.bfloat16)
    head_out = head_out.reshape(count, HEADS * HD)
    passed = (inputs.astype(jnp.float32) + jnp.dot(head_out, out_weight, preferred_element_type=jnp.float32)).astype(jnp.bfloat16)

    def add_block(running, block):
        keys_block, values_block, rates_block = block
        term = group_terms(keys_block, values_block, rates_block, gate_fast, up_fast, down_fast)
        return (running + to_half(term), None)
    blocks = (key_rows.reshape(N_CTX, -1, HEADS, HD), value_rows.reshape(N_CTX, -1, HEADS, HD), rates.reshape(N_CTX, -1, HEADS))
    gradient, _ = lax.scan(add_block, jnp.zeros((3, HEADS, FH, HD), jnp.float32), blocks)
    current = orthogonalize(gradient)
    stepped = fast_state - update_scale * current
    rescale = jnp.sqrt(lax.optimization_barrier(jnp.mean(fast_state * fast_state, axis=-1, keepdims=True)) + 1e-06) * lax.rsqrt(lax.optimization_barrier(jnp.mean(stepped * stepped, axis=-1, keepdims=True)) + 1e-06)
    return (passed, stepped * rescale)

def reference(fresh_input, carried, qkv_weight, out_weight, rate_weight, fast_state):
    passed_rows = []
    state_rows = []
    for section in range(N_SEC):
        for sequence in range(N_DP):
            if section == 0:
                inputs = fresh_input[sequence]
            else:
                inputs = carried[section - 1, sequence]
            passed, updated = fast_layer(inputs, qkv_weight[section], out_weight[section], rate_weight[section], fast_state[section, sequence])
            passed_rows.append(passed)
            state_rows.append(updated)
    passed_all = jnp.stack(passed_rows).reshape(N_SEC, N_DP, GROUP, D)
    state_all = jnp.stack(state_rows).reshape(N_SEC, N_DP, 3, HEADS, FH, HD)
    return (passed_all, state_all)
```

```python
import jax
import jax.numpy as jnp
from jax import lax
from jax.sharding import PartitionSpec as P

NS_STEPS = 2


linear_coef = 3.4445
cubic_coef = -4.775
quintic_coef = 2.0315
update_scale = 8.0
highest = lax.Precision.HIGHEST


def from_behind(block, axis, distance):
    devices = range(lax.axis_size(axis))
    route = [(i - distance, i) for i in devices if i - distance in devices]
    return lax.ppermute(block, axis, route)


def swish(values):
    return values * jax.nn.sigmoid(values)


def unit_rows(values):
    return values / jnp.sqrt(jnp.sum(values * values, axis=-1, keepdims=True) + 1e-06)


def head_slots(heads):
    devices = lax.axis_size("ctx")
    each = -(-heads // devices)
    return devices * each


def pad_axis(block, axis, size):
    widths = [(0, 0)] * block.ndim
    widths[axis] = (0, size - block.shape[axis])
    return jnp.pad(block, widths)


def exchange(block, split, concat):
    return lax.all_to_all(block, "ctx", split_axis=split, concat_axis=concat, tiled=True)


def matmul_tn(a, b, precision=None):
    return lax.dot_general(
        a, b, (((0,), (0,)), ((), ())), preferred_element_type=jnp.float32, precision=precision
    )


def orthogonalize(gradient):
    square = matmul_tn(gradient, gradient, highest)
    inverse_norm = lax.rsqrt(jnp.trace(square) + 1e-06)
    square = square * inverse_norm * inverse_norm
    eye = jnp.eye(square.shape[0], dtype=jnp.float32)
    total = None
    for iteration in range(NS_STEPS):
        quad = jnp.dot(square, square, precision=highest)
        poly = linear_coef * eye + cubic_coef * square + quintic_coef * quad
        total = poly if total is None else jnp.dot(total, poly, precision=highest)
        if iteration + 1 < NS_STEPS:
            square = jnp.dot(
                jnp.dot(poly, square, precision=highest), poly, precision=highest
            )
    return jnp.dot(gradient * inverse_norm, total, precision=highest)


def head_terms(inputs, weight, rate_weight, fast):
    head_dim = fast.shape[2]
    projected = jnp.dot(inputs, weight, preferred_element_type=jnp.float32)
    rates = jax.nn.softplus(
        jnp.dot(inputs, rate_weight[:, None], preferred_element_type=jnp.float32)
    )
    query_rows = unit_rows(swish(projected[:, :head_dim])).astype(jnp.bfloat16)
    key_rows = unit_rows(swish(projected[:, head_dim : 2 * head_dim])).astype(jnp.bfloat16)
    value_rows = projected[:, 2 * head_dim :].astype(jnp.bfloat16)
    gate_fast, up_fast, down_fast = fast[0], fast[1], fast[2]

    def dot_nt(a, b):
        return lax.dot_general(
            a, b, (((1,), (1,)), ((), ())), preferred_element_type=jnp.float32
        )

    gate_query = dot_nt(query_rows, gate_fast)
    up_query = dot_nt(query_rows, up_fast)
    hidden = (swish(gate_query) * up_query).astype(jnp.bfloat16)
    mixture = jnp.dot(hidden, down_fast, preferred_element_type=jnp.float32)
    head_out = (
        mixture * lax.rsqrt(jnp.mean(mixture * mixture, axis=-1, keepdims=True) + 1e-05)
    ).astype(jnp.bfloat16)
    gate_pre = dot_nt(key_rows, gate_fast)
    up_pre = dot_nt(key_rows, up_fast)
    sigma = jax.nn.sigmoid(gate_pre)
    gate_act = gate_pre * sigma
    key_hidden = (gate_act * up_pre).astype(jnp.bfloat16)
    scaled_values = (rates * value_rows.astype(jnp.float32)).astype(jnp.bfloat16)
    hidden_grad = -dot_nt(scaled_values, down_fast)
    up_grad = (hidden_grad * gate_act).astype(jnp.bfloat16)
    gate_grad = (hidden_grad * up_pre * sigma * (1.0 + gate_pre * (1.0 - sigma))).astype(
        jnp.bfloat16
    )
    update = jnp.stack(
        [
            orthogonalize(matmul_tn(gate_grad, key_rows)),
            orthogonalize(matmul_tn(up_grad, key_rows)),
            orthogonalize(-matmul_tn(key_hidden, scaled_values)),
        ]
    )
    return head_out, update.astype(jnp.bfloat16)


def local(fresh_input, carried, qkv_weight, out_weight, rate_weight, fast_state):
    received = from_behind(carried, "sec", 1)
    is_first = lax.axis_index("sec") == 0
    inputs = jnp.where(is_first, fresh_input[None], received)[0, 0]
    heads = rate_weight.shape[2]
    head_dim = fast_state.shape[5]
    depth = rate_weight.shape[1]
    previous = fast_state[0, 0]
    slots = head_slots(heads)
    each = slots // lax.axis_size("ctx")

    all_inputs = lax.all_gather(inputs, "ctx", axis=0, tiled=True)
    full_out = lax.all_gather(out_weight[0], ("ctx", "dp"), axis=0, tiled=True)
    full_rate = lax.all_gather(rate_weight[0], ("ctx", "dp"), axis=0, tiled=True)

    fast = exchange(pad_axis(previous.astype(jnp.bfloat16), 1, slots), 1, 2)
    columns = qkv_weight[0].reshape(depth, 3, heads, head_dim).transpose(2, 0, 1, 3)
    columns = columns.reshape(heads, depth, 3 * head_dim)
    columns = exchange(pad_axis(columns, 0, slots), 0, 1)
    columns = lax.all_gather(
        columns.reshape(each, lax.axis_size("ctx"), depth, 3 * head_dim), "dp", axis=2, tiled=True
    ).reshape(each, -1, 3 * head_dim)
    first = lax.axis_index("ctx") * each
    rate_columns = lax.dynamic_slice_in_dim(pad_axis(full_rate, 1, slots), first, each, 1)

    outs, updates = [], []
    for slot in range(each):
        head_out, update = head_terms(
            all_inputs, columns[slot], rate_columns[:, slot], fast[:, slot]
        )
        outs.append(head_out)
        updates.append(update)
    head_out = exchange(jnp.concatenate(outs, axis=1), 0, 1)[:, : heads * head_dim]
    branch_out = jnp.dot(head_out, full_out, preferred_element_type=jnp.float32)
    passed = (inputs.astype(jnp.float32) + branch_out).astype(jnp.bfloat16)

    update = exchange(jnp.stack(updates, axis=1), 2, 1)[:, :heads]
    stepped = previous - update_scale * update.astype(jnp.float32)
    rescale = jnp.sqrt(jnp.mean(previous * previous, axis=-1, keepdims=True) + 1e-06) * lax.rsqrt(
        jnp.mean(stepped * stepped, axis=-1, keepdims=True) + 1e-06
    )
    new_state = (stepped * rescale)[None, None]
    return (passed[None, None], new_state)


def solution(mesh):
    in_specs = (
        P("dp", "ctx", None),
        P("sec", "dp", "ctx", None),
        P("sec", ("ctx", "dp"), None),
        P("sec", ("ctx", "dp"), None),
        P("sec", ("ctx", "dp"), None),
        P("sec", "dp", None, None, "ctx", None),
    )
    out_specs = (P("sec", "dp", "ctx", None), P("sec", "dp", None, None, "ctx", None))
    return jax.shard_map(local, mesh=mesh, in_specs=in_specs, out_specs=out_specs, check_vma=False)
```

```python
import functools

import jax
import jax.numpy as jnp
from jax import lax
from jax.experimental import pallas as pl
from jax.experimental.pallas import tpu as pltpu
from jax.sharding import PartitionSpec as P

NS_STEPS = 2
LANES = 128
PAIR = 2
VMEM_BYTES = 56 * 2**20

linear_coef = 3.4445
cubic_coef = -4.775
quintic_coef = 2.0315
update_scale = 8.0
highest = lax.Precision.HIGHEST
MESH = pl.DeviceIdType.MESH


def swish(values):
    return values * jax.nn.sigmoid(values)


def unit_rows(values):
    return values * lax.rsqrt(jnp.sum(values * values, axis=-1, keepdims=True) + 1e-06)


def dot_nn(a, b, precision=None):
    return jnp.dot(a, b, preferred_element_type=jnp.float32, precision=precision)


def dot_nt(a, b):
    return lax.dot_general(a, b, (((1,), (1,)), ((), ())), preferred_element_type=jnp.float32)


def dot_tn(a, b, precision=None):
    return lax.dot_general(
        a, b, (((0,), (0,)), ((), ())), preferred_element_type=jnp.float32, precision=precision
    )


def orthogonalize(gradient):
    square = dot_tn(gradient, gradient, highest)
    rows = lax.broadcasted_iota(jnp.int32, square.shape, 0)
    columns = lax.broadcasted_iota(jnp.int32, square.shape, 1)
    eye = (rows == columns).astype(jnp.float32)
    trace = jnp.sum(jnp.sum(square * eye, axis=1, keepdims=True), axis=0, keepdims=True)
    inverse_norm = lax.rsqrt(trace + 1e-06)
    square = square * inverse_norm * inverse_norm
    total = None
    for iteration in range(NS_STEPS):
        quad = dot_nn(square, square, highest)
        poly = linear_coef * eye + cubic_coef * square + quintic_coef * quad
        total = poly if total is None else dot_nn(total, poly, highest)
        if iteration + 1 < NS_STEPS:
            square = dot_nn(dot_nn(poly, square, highest), poly, highest)
    return dot_nn(gradient * inverse_norm, total, highest)


def block_terms(inputs, weight_ref, fast_ref, gradient_ref):
    head_dim = fast_ref.shape[2]
    weight = weight_ref[...].reshape(inputs.shape[1], weight_ref.shape[3])
    projected = dot_nn(inputs, weight)
    query_rows = unit_rows(swish(projected[:, :head_dim])).astype(jnp.bfloat16)
    key_rows = unit_rows(swish(projected[:, head_dim : 2 * head_dim])).astype(jnp.bfloat16)
    value_rows = projected[:, 2 * head_dim : 3 * head_dim].astype(jnp.bfloat16)
    rates = jax.nn.softplus(projected[:, 3 * head_dim : 3 * head_dim + 1])
    scaled_values = (rates * value_rows.astype(jnp.float32)).astype(jnp.bfloat16)

    gate_query = dot_nt(query_rows, fast_ref[0])
    up_query = dot_nt(query_rows, fast_ref[1])
    hidden = (swish(gate_query) * up_query).astype(jnp.bfloat16)
    mixture = dot_nn(hidden, fast_ref[2])
    head_out = mixture * lax.rsqrt(jnp.mean(mixture * mixture, axis=-1, keepdims=True) + 1e-05)

    gate_pre = dot_nt(key_rows, fast_ref[0])
    up_pre = dot_nt(key_rows, fast_ref[1])
    sigma = jax.nn.sigmoid(gate_pre)
    gate_act = gate_pre * sigma
    key_hidden = (gate_act * up_pre).astype(jnp.bfloat16)
    hidden_grad = -dot_nt(scaled_values, fast_ref[2])
    up_grad = (hidden_grad * gate_act).astype(jnp.bfloat16)
    gate_grad = (hidden_grad * up_pre * sigma * (1.0 + gate_pre * (1.0 - sigma))).astype(
        jnp.bfloat16
    )
    gradient_ref[0] += dot_tn(gate_grad, key_rows)
    gradient_ref[1] += dot_tn(up_grad, key_rows)
    gradient_ref[2] -= dot_tn(key_hidden, scaled_values)
    return head_out.astype(jnp.bfloat16)


def kernel(
    sizes, fresh, carried, columns, fast_rows, inputs_out, head_out, update_out,
    blocks, weight, fast, gradient, out_stage, out_land, update_stage, update_land,
    y_sem, load_sem, own_sem, w_send, w_recv, f_send, f_recv, d_send, d_recv,
    up_send, down_send, line_recv, pair_send, pair_recv, h_send, h_recv, u_send, u_recv,
):
    n_ctx, n_sec, n_dp, heads = sizes
    lines = n_ctx // PAIR
    me = lax.axis_index("ctx")
    sec = lax.axis_index("sec")
    dp = lax.axis_index("dp")
    line, side = me // PAIR, lax.rem(me, PAIR)
    hidden_rows = fast_rows.shape[2]
    head_dim = fast_rows.shape[3]
    owner = me < heads
    from_sec = sec > 0
    to_sec = sec + 1 < n_sec

    def remote(src, dst, send, recv, **device):
        return pltpu.make_async_remote_copy(
            src_ref=src, dst_ref=dst, send_sem=send, recv_sem=recv,
            device_id=device, device_id_type=MESH,
        )

    def peer(step):
        return lax.rem(me + step, n_ctx)

    barrier = pltpu.get_barrier_semaphore()
    for step in range(1, n_ctx):
        pl.semaphore_signal(barrier, inc=1, device_id={"ctx": peer(step)}, device_id_type=MESH)
    for step in range(1, n_dp):
        pl.semaphore_signal(
            barrier, inc=1, device_id={"dp": lax.rem(dp + step, n_dp)}, device_id_type=MESH
        )

    for step in range(1, n_sec):
        pl.semaphore_signal(
            barrier, inc=1, device_id={"sec": lax.rem(sec + step, n_sec)}, device_id_type=MESH
        )
    pl.semaphore_wait(barrier, n_ctx + n_dp + n_sec - 3)

    def y_copy():
        return remote(
            carried.at[0, 0], blocks.at[me], y_sem.at[0], y_sem.at[1], sec=lax.rem(sec + 1, n_sec)
        )

    def fresh_copy():
        return pltpu.make_async_copy(fresh.at[0], blocks.at[me], load_sem)

    @pl.when(to_sec)
    def _():
        y_copy().start()

    @pl.when(sec == 0)
    def _():
        fresh_copy().start()

    my_rows = pl.ds(pl.multiple_of(me * hidden_rows, hidden_rows), hidden_rows)

    def w_copy(target):
        return remote(
            columns.at[target], weight.at[me, dp], w_send.at[target], w_recv.at[me], ctx=target
        )

    def f_copy(target):
        return remote(
            fast_rows.at[:, target], fast.at[:, my_rows], f_send.at[target], f_recv.at[me],
            ctx=target,
        )

    def own_copies():
        return (
            pltpu.make_async_copy(columns.at[me], weight.at[me, dp], own_sem.at[0]),
            pltpu.make_async_copy(fast_rows.at[:, me], fast.at[:, my_rows], own_sem.at[1]),
        )

    for step in range(1, n_ctx):
        target = peer(step)

        @pl.when(target < heads)
        def _():
            w_copy(target).start()

    for step in range(1, n_ctx):
        target = peer(step)

        @pl.when(target < heads)
        def _():
            f_copy(target).start()

    @pl.when(owner)
    def _():
        for copy in own_copies():
            copy.start()
        gradient[...] = jnp.zeros_like(gradient)

    def shard(row, which):
        return row * PAIR + which

    def line_copy(row, sem, to_line):
        at = shard(row, side)
        return remote(
            blocks.at[at], blocks.at[at], sem.at[row], line_recv.at[row],
            ctx=shard(to_line, side),
        )

    def pair_copy(row):
        at = shard(row, side)
        return remote(
            blocks.at[at], blocks.at[at], pair_send.at[row], pair_recv.at[row],
            ctx=shard(line, 1 - side),
        )

    def pass_on(row, distance, sign):
        @pl.when(distance > 0)
        def _():
            remote(
                blocks.at[shard(row, side)], blocks.at[shard(row, side)],
                up_send.at[row], line_recv.at[row], ctx=peer(1),
            ).wait_recv()

        @pl.when((row <= line) & (line + 1 < lines))
        def _():
            line_copy(row, up_send, line + 1).start()

        @pl.when((row >= line) & (line > 0))
        def _():
            line_copy(row, down_send, line - 1).start()

        pair_copy(row).start()

    def out_copy(at):
        return remote(
            out_stage.at[at], out_land.at[me], h_send.at[at], h_recv.at[me], ctx=at
        )

    def compute(at):
        out = block_terms(blocks[at], weight, fast, gradient)

        @pl.when(at == me)
        def _():
            out_land[me] = out

        @pl.when(at != me)
        def _():
            out_stage[at] = out
            out_copy(at).start()

    def rows_at(distance, sign):
        row = line + distance * (1 - 2 * sign)
        valid = (row >= 0) & (row < lines) & ((distance > 0) | (sign == 0))
        return row, valid

    @pl.when(sec == 0)
    def _():
        fresh_copy().wait()

    @pl.when(from_sec)
    def _():
        y_copy().wait_recv()

    def weights_ready():
        @pl.when(owner)
        def _():
            for step in range(1, n_ctx):
                source = peer(step)
                remote(
                    columns.at[0], weight.at[source, dp], w_send.at[0], w_recv.at[source],
                    ctx=source,
                ).wait_recv()
            for copy in own_copies():
                copy.wait()
            for step in range(1, n_dp):
                remote(
                    weight.at[:, dp], weight.at[:, dp], d_send.at[step], d_recv.at[step],
                    dp=lax.rem(dp + step, n_dp),
                ).start()
            for step in range(1, n_ctx):
                source = peer(step)
                rows = pl.ds(pl.multiple_of(source * hidden_rows, hidden_rows), hidden_rows)
                remote(
                    fast_rows.at[:, 0], fast.at[:, rows], f_send.at[0], f_recv.at[source],
                    ctx=source,
                ).wait_recv()
            for step in range(1, n_dp):
                source = lax.rem(dp + n_dp - step, n_dp)
                remote(
                    weight.at[:, source], weight.at[:, source], d_send.at[step], d_recv.at[step],
                    dp=source,
                ).wait()

    def step_body(distance, carry):
        @pl.when(distance < lines)
        def _():
            for sign in range(2):
                row, valid = rows_at(distance, sign)

                @pl.when(valid)
                def _():
                    pass_on(row, distance, sign)

        @pl.when(distance == 1)
        def _():
            weights_ready()

        @pl.when(distance > 0)
        def _():
            def block_body(index, inner):
                sign, far = index // 2, lax.rem(index, 2)
                row, valid = rows_at(distance - 1, sign)

                @pl.when(valid)
                def _():
                    at = shard(row, lax.rem(side + far, 2))

                    @pl.when(far == 1)
                    def _():
                        remote(
                            blocks.at[at], blocks.at[at], pair_send.at[row], pair_recv.at[row],
                            ctx=shard(line, 1 - side),
                        ).wait_recv()

                    @pl.when(owner)
                    def _():
                        compute(at)

                return inner

            lax.fori_loop(0, 4, block_body, 0)

        return carry

    lax.fori_loop(0, lines + 1, step_body, 0)

    def update_copy(target):
        rows = pl.ds(pl.multiple_of(target * hidden_rows, hidden_rows), hidden_rows)
        return remote(
            update_stage.at[:, rows], update_land.at[:, me], u_send.at[target], u_recv.at[me],
            ctx=target,
        )

    @pl.when(owner)
    def _():
        def matrix_body(which, carry):
            update_stage[which] = orthogonalize(gradient[which]).astype(jnp.bfloat16)
            return carry

        lax.fori_loop(0, 3, matrix_body, 0)
        for step in range(1, n_ctx):
            update_copy(peer(step)).start()
        update_land[:, me] = update_stage[:, my_rows]

    inputs_out[...] = blocks[me]
    for head in range(heads):
        @pl.when(me != head)
        def _():
            remote(
                out_stage.at[0], out_land.at[head], h_send.at[0], h_recv.at[head], ctx=head
            ).wait_recv()

        head_out[:, head * head_dim : (head + 1) * head_dim] = out_land[head]
    for head in range(heads):
        @pl.when(me != head)
        def _():
            remote(
                update_stage.at[:, pl.ds(0, hidden_rows)], update_land.at[:, head],
                u_send.at[0], u_recv.at[head], ctx=head,
            ).wait_recv()

    update_out[...] = update_land[:, :heads]

    @pl.when(to_sec)
    def _():
        y_copy().wait_send()

    for step in range(1, n_ctx):
        target = peer(step)

        @pl.when(target < heads)
        def _():
            w_copy(target).wait_send()
            f_copy(target).wait_send()

        @pl.when(owner)
        def _():
            out_copy(target).wait_send()
            update_copy(target).wait_send()

    for row in range(lines):
        @pl.when((row <= line) & (line + 1 < lines))
        def _():
            line_copy(row, up_send, lax.rem(line + 1, lines)).wait_send()

        @pl.when((row >= line) & (line > 0))
        def _():
            line_copy(row, down_send, lax.rem(line + lines - 1, lines)).wait_send()

        pair_copy(row).wait_send()


def local(fresh_input, carried, qkv_weight, out_weight, rate_weight, fast_state):
    n_ctx, n_sec, n_dp = (lax.axis_size(axis) for axis in ("ctx", "sec", "dp"))
    heads = rate_weight.shape[2]
    head_dim = fast_state.shape[5]
    hidden_rows = fast_state.shape[4]
    depth = rate_weight.shape[1]
    count, width = fresh_input.shape[1:]
    assert heads <= n_ctx and n_ctx % PAIR == 0
    previous = fast_state[0, 0]
    full_out = lax.all_gather(out_weight[0], ("ctx", "dp"), axis=0, tiled=True)

    columns = qkv_weight[0].reshape(depth, 3, heads, head_dim).transpose(2, 0, 1, 3)
    columns = columns.reshape(heads, depth, 3 * head_dim)
    rate_columns = jnp.pad(rate_weight[0].T[:, :, None], ((0, 0), (0, 0), (0, LANES - 1)))
    columns = jnp.concatenate([columns, rate_columns], axis=2)
    fast_rows = previous.astype(jnp.bfloat16)

    half = jnp.bfloat16
    dma = pltpu.SemaphoreType.DMA
    lines = n_ctx // PAIR
    any_spec = pl.BlockSpec(memory_space=pl.ANY)
    vmem_spec = pl.BlockSpec(memory_space=pltpu.VMEM)
    tokens = n_ctx * count
    hidden_all = n_ctx * hidden_rows
    flops = 2 * tokens * head_dim * (3 * width + 9 * hidden_all)
    inputs, head_out, update = pl.pallas_call(
        functools.partial(kernel, (n_ctx, n_sec, n_dp, heads)),
        out_shape=[
            jax.ShapeDtypeStruct((count, width), half),
            jax.ShapeDtypeStruct((count, heads * head_dim), half),
            jax.ShapeDtypeStruct((3, heads, hidden_rows, head_dim), half),
        ],
        in_specs=[any_spec] * 4,
        out_specs=[vmem_spec] * 3,
        scratch_shapes=[
            pltpu.VMEM((n_ctx, count, width), half),
            pltpu.VMEM((n_ctx, n_dp, depth, 3 * head_dim + LANES), half),
            pltpu.VMEM((3, hidden_all, head_dim), half),
            pltpu.VMEM((3, hidden_all, head_dim), jnp.float32),
            pltpu.VMEM((n_ctx, count, head_dim), half),
            pltpu.VMEM((n_ctx, count, head_dim), half),
            pltpu.VMEM((3, hidden_all, head_dim), half),
            pltpu.VMEM((3, n_ctx, hidden_rows, head_dim), half),
            dma((2,)), dma, dma((2,)),
            dma((n_ctx,)), dma((n_ctx,)), dma((n_ctx,)), dma((n_ctx,)),
            dma((n_dp,)), dma((n_dp,)),
            dma((lines,)), dma((lines,)), dma((lines,)), dma((lines,)), dma((lines,)),
            dma((n_ctx,)), dma((n_ctx,)), dma((n_ctx,)), dma((n_ctx,)),
        ],
        compiler_params=pltpu.CompilerParams(
            collective_id=0, has_side_effects=True, vmem_limit_bytes=VMEM_BYTES
        ),
        cost_estimate=pl.CostEstimate(
            flops=flops, bytes_accessed=tokens * width * 2, transcendentals=4 * tokens * hidden_all
        ),
    )(fresh_input, carried, columns, fast_rows)

    branch_out = jnp.dot(head_out, full_out, preferred_element_type=jnp.float32)
    passed = (inputs.astype(jnp.float32) + branch_out).astype(jnp.bfloat16)
    stepped = previous - update_scale * update.astype(jnp.float32)
    rescale = jnp.sqrt(jnp.mean(previous * previous, axis=-1, keepdims=True) + 1e-06) * lax.rsqrt(
        jnp.mean(stepped * stepped, axis=-1, keepdims=True) + 1e-06
    )
    new_state = (stepped * rescale)[None, None]
    return (passed[None, None], new_state)


def solution(mesh):
    in_specs = (
        P("dp", "ctx", None),
        P("sec", "dp", "ctx", None),
        P("sec", ("ctx", "dp"), None),
        P("sec", ("ctx", "dp"), None),
        P("sec", ("ctx", "dp"), None),
        P("sec", "dp", None, None, "ctx", None),
    )
    out_specs = (P("sec", "dp", "ctx", None), P("sec", "dp", None, None, "ctx", None))
    return jax.shard_map(local, mesh=mesh, in_specs=in_specs, out_specs=out_specs, check_vma=False)
```

```python
import functools

import jax
import jax.numpy as jnp
from jax import lax
from jax.experimental import pallas as pl
from jax.experimental.pallas import tpu as pltpu
from jax.sharding import PartitionSpec as P

NS_STEPS = 2
LANES = 128
PAIR = 2
VMEM_BYTES = 56 * 2**20

linear_coef = 3.4445
cubic_coef = -4.775
quintic_coef = 2.0315
update_scale = 8.0
MESH = pl.DeviceIdType.MESH


def swish(values):
    return values * jax.nn.sigmoid(values)


def unit_rows(values):
    return values * lax.rsqrt(jnp.sum(values * values, axis=-1, keepdims=True) + 1e-06)


def dot_nn(a, b):
    return jnp.dot(a, b, preferred_element_type=jnp.float32)


def dot_nt(a, b):
    return lax.dot_general(a, b, (((1,), (1,)), ((), ())), preferred_element_type=jnp.float32)


def dot_tn(a, b):
    return lax.dot_general(a, b, (((0,), (0,)), ((), ())), preferred_element_type=jnp.float32)


def parts_of(values):
    high = values.astype(jnp.bfloat16)
    return high, (values - high.astype(jnp.float32)).astype(jnp.bfloat16)


def dot_split(dot, a, b):
    return dot(a[0], b[0]) + (dot(a[0], b[1]) + dot(a[1], b[0]))


def orthogonalize(gradient):
    gradient_parts = parts_of(gradient)
    square = dot_split(dot_tn, gradient_parts, gradient_parts)
    rows = lax.broadcasted_iota(jnp.int32, square.shape, 0)
    columns = lax.broadcasted_iota(jnp.int32, square.shape, 1)
    eye = (rows == columns).astype(jnp.float32)
    trace = jnp.sum(jnp.sum(square * eye, axis=1, keepdims=True), axis=0, keepdims=True)
    inverse_norm = lax.rsqrt(trace + 1e-06)
    square = square * inverse_norm * inverse_norm
    total = None
    for iteration in range(NS_STEPS):
        square_parts = parts_of(square)
        quad = dot_split(dot_nn, square_parts, square_parts)
        poly = linear_coef * eye + cubic_coef * square + quintic_coef * quad
        poly_parts = parts_of(poly)
        if total is None:
            total = poly
        else:
            total = dot_split(dot_nn, parts_of(total), poly_parts)
        if iteration + 1 < NS_STEPS:
            left = dot_split(dot_nn, poly_parts, square_parts)
            square = dot_split(dot_nn, parts_of(left), poly_parts)
    return dot_split(dot_nn, gradient_parts, parts_of(total * inverse_norm))


def block_terms(inputs, weight_ref, fast_ref, gradient_ref):
    head_dim = fast_ref.shape[2]
    weight = weight_ref[...].reshape(inputs.shape[1], weight_ref.shape[3])
    projected = dot_nn(inputs, weight)
    query_rows = unit_rows(swish(projected[:, :head_dim])).astype(jnp.bfloat16)
    key_rows = unit_rows(swish(projected[:, head_dim : 2 * head_dim])).astype(jnp.bfloat16)
    value_rows = projected[:, 2 * head_dim : 3 * head_dim].astype(jnp.bfloat16)
    rates = jax.nn.softplus(projected[:, 3 * head_dim : 3 * head_dim + 1])
    scaled_values = (rates * value_rows.astype(jnp.float32)).astype(jnp.bfloat16)

    gate_query = dot_nt(query_rows, fast_ref[0])
    up_query = dot_nt(query_rows, fast_ref[1])
    hidden = (swish(gate_query) * up_query).astype(jnp.bfloat16)
    mixture = dot_nn(hidden, fast_ref[2])
    head_out = mixture * lax.rsqrt(jnp.mean(mixture * mixture, axis=-1, keepdims=True) + 1e-05)

    gate_pre = dot_nt(key_rows, fast_ref[0])
    up_pre = dot_nt(key_rows, fast_ref[1])
    sigma = jax.nn.sigmoid(gate_pre)
    gate_act = gate_pre * sigma
    key_hidden = (gate_act * up_pre).astype(jnp.bfloat16)
    hidden_grad = -dot_nt(scaled_values, fast_ref[2])
    up_grad = (hidden_grad * gate_act).astype(jnp.bfloat16)
    gate_grad = (hidden_grad * up_pre * sigma * (1.0 + gate_pre * (1.0 - sigma))).astype(
        jnp.bfloat16
    )
    gradient_ref[0] += dot_tn(gate_grad, key_rows)
    gradient_ref[1] += dot_tn(up_grad, key_rows)
    gradient_ref[2] -= dot_tn(key_hidden, scaled_values)
    return head_out.astype(jnp.bfloat16)


def kernel(
    sizes, fresh, carried, columns, fast_rows, out_rows, passed_out, update_out,
    blocks, weight, fast, gradient, out_stage, out_land, update_stage, update_land, projection,
    y_sem, load_sem, own_sem, w_send, w_recv, f_send, f_recv, d_send, d_recv,
    up_send, down_send, line_recv, pair_send, pair_recv, h_send, h_recv, u_send, u_recv,
    o_load, o_up_send, o_down_send, o_line_recv, o_pair_send, o_pair_recv, o_core_send, o_core_recv,
):
    n_ctx, n_sec, n_dp, heads = sizes
    lines = n_ctx // PAIR
    me = lax.axis_index("ctx")
    sec = lax.axis_index("sec")
    dp = lax.axis_index("dp")
    line, side = me // PAIR, lax.rem(me, PAIR)
    hidden_rows = fast_rows.shape[2]
    head_dim = fast_rows.shape[3]
    owner = me < heads
    from_sec = sec > 0
    to_sec = sec + 1 < n_sec

    def remote(src, dst, send, recv, **device):
        return pltpu.make_async_remote_copy(
            src_ref=src, dst_ref=dst, send_sem=send, recv_sem=recv,
            device_id=device, device_id_type=MESH,
        )

    def peer(step):
        return lax.rem(me + step, n_ctx)

    barrier = pltpu.get_barrier_semaphore()
    for step in range(1, n_ctx):
        pl.semaphore_signal(barrier, inc=1, device_id={"ctx": peer(step)}, device_id_type=MESH)
    for step in range(1, n_dp):
        pl.semaphore_signal(
            barrier, inc=1, device_id={"dp": lax.rem(dp + step, n_dp)}, device_id_type=MESH
        )

    for step in range(1, n_sec):
        pl.semaphore_signal(
            barrier, inc=1, device_id={"sec": lax.rem(sec + step, n_sec)}, device_id_type=MESH
        )
    pl.semaphore_wait(barrier, n_ctx + n_dp + n_sec - 3)

    def y_copy():
        return remote(
            carried.at[0, 0], blocks.at[me], y_sem.at[0], y_sem.at[1], sec=lax.rem(sec + 1, n_sec)
        )

    def fresh_copy():
        return pltpu.make_async_copy(fresh.at[0], blocks.at[me], load_sem)

    @pl.when(to_sec)
    def _():
        y_copy().start()

    @pl.when(sec == 0)
    def _():
        fresh_copy().start()

    my_rows = pl.ds(pl.multiple_of(me * hidden_rows, hidden_rows), hidden_rows)

    def w_copy(target):
        return remote(
            columns.at[target], weight.at[me, dp], w_send.at[target], w_recv.at[me], ctx=target
        )

    def f_copy(target):
        return remote(
            fast_rows.at[:, target], fast.at[:, my_rows], f_send.at[target], f_recv.at[me],
            ctx=target,
        )

    def own_copies():
        return (
            pltpu.make_async_copy(columns.at[me], weight.at[me, dp], own_sem.at[0]),
            pltpu.make_async_copy(fast_rows.at[:, me], fast.at[:, my_rows], own_sem.at[1]),
        )

    for step in range(1, n_ctx):
        target = peer(step)

        @pl.when(target < heads)
        def _():
            w_copy(target).start()

    for step in range(1, n_ctx):
        target = peer(step)

        @pl.when(target < heads)
        def _():
            f_copy(target).start()

    def own_projection():
        return pltpu.make_async_copy(out_rows.at[0], projection.at[me, dp], o_load)

    own_projection().start()

    @pl.when(owner)
    def _():
        for copy in own_copies():
            copy.start()
        gradient[...] = jnp.zeros_like(gradient)

    def shard(row, which):
        return row * PAIR + which

    def input_slot(at):
        return blocks.at[at]

    def projection_slot(at):
        return projection.at[at, dp]

    input_relay = (input_slot, up_send, down_send, line_recv, pair_send, pair_recv)
    projection_relay = (
        projection_slot, o_up_send, o_down_send, o_line_recv, o_pair_send, o_pair_recv
    )

    def up_copy(relay, row):
        slot = relay[0](shard(row, side))
        to = shard(lax.rem(line + 1, lines), side)
        return remote(slot, slot, relay[1].at[row], relay[3].at[row], ctx=to)

    def down_copy(relay, row):
        slot = relay[0](shard(row, side))
        to = shard(lax.rem(line + lines - 1, lines), side)
        return remote(slot, slot, relay[2].at[row], relay[3].at[row], ctx=to)

    def pair_copy(relay, row):
        slot = relay[0](shard(row, side))
        to = shard(line, 1 - side)
        return remote(slot, slot, relay[4].at[row], relay[5].at[row], ctx=to)

    def pair_arrived(relay, row):
        slot = relay[0](shard(row, 1 - side))
        to = shard(line, 1 - side)
        remote(slot, slot, relay[4].at[row], relay[5].at[row], ctx=to).wait_recv()

    def pass_on(relay, row, distance):
        @pl.when(distance > 0)
        def _():
            up_copy(relay, row).wait_recv()

        @pl.when((row <= line) & (line + 1 < lines))
        def _():
            up_copy(relay, row).start()

        @pl.when((row >= line) & (line > 0))
        def _():
            down_copy(relay, row).start()

        pair_copy(relay, row).start()

    def relay_sent(relay):
        for row in range(lines):
            @pl.when((row <= line) & (line + 1 < lines))
            def _():
                up_copy(relay, row).wait_send()

            @pl.when((row >= line) & (line > 0))
            def _():
                down_copy(relay, row).wait_send()

            pair_copy(relay, row).wait_send()

    def out_copy(at):
        return remote(
            out_stage.at[at], out_land.at[me], h_send.at[at], h_recv.at[me], ctx=at
        )

    def compute(row):
        first = row * PAIR
        tokens = blocks[pl.ds(first, PAIR)].reshape(PAIR * blocks.shape[1], blocks.shape[2])
        out = block_terms(tokens, weight, fast, gradient)
        for which in range(PAIR):
            at = first + which
            part = out[which * blocks.shape[1] : (which + 1) * blocks.shape[1]]

            @pl.when(at == me)
            def _():
                out_land[me] = part

            @pl.when(at != me)
            def _():
                out_stage[at] = part
                out_copy(at).start()

    def rows_at(distance, sign):
        row = line + distance * (1 - 2 * sign)
        valid = (row >= 0) & (row < lines) & ((distance > 0) | (sign == 0))
        return row, valid

    @pl.when(sec == 0)
    def _():
        fresh_copy().wait()

    @pl.when(from_sec)
    def _():
        y_copy().wait_recv()

    def weights_ready():
        @pl.when(owner)
        def _():
            for step in range(1, n_ctx):
                source = peer(step)
                remote(
                    columns.at[0], weight.at[source, dp], w_send.at[0], w_recv.at[source],
                    ctx=source,
                ).wait_recv()
            for copy in own_copies():
                copy.wait()
            for step in range(1, n_dp):
                remote(
                    weight.at[:, dp], weight.at[:, dp], d_send.at[step], d_recv.at[step],
                    dp=lax.rem(dp + step, n_dp),
                ).start()
            for step in range(1, n_ctx):
                source = peer(step)
                rows = pl.ds(pl.multiple_of(source * hidden_rows, hidden_rows), hidden_rows)
                remote(
                    fast_rows.at[:, 0], fast.at[:, rows], f_send.at[0], f_recv.at[source],
                    ctx=source,
                ).wait_recv()
            for step in range(1, n_dp):
                source = lax.rem(dp + n_dp - step, n_dp)
                remote(
                    weight.at[:, source], weight.at[:, source], d_send.at[step], d_recv.at[step],
                    dp=source,
                ).wait()

    def step_body(distance, carry):
        @pl.when(distance < lines)
        def _():
            for sign in range(2):
                row, valid = rows_at(distance, sign)

                @pl.when(valid)
                def _():
                    pass_on(input_relay, row, distance)

        @pl.when(distance == 1)
        def _():
            weights_ready()
            own_projection().wait()

        @pl.when(distance > 0)
        def _():
            def block_body(sign, inner):
                row, valid = rows_at(distance - 1, sign)

                @pl.when(valid)
                def _():
                    pair_arrived(input_relay, row)

                    @pl.when(owner)
                    def _():
                        compute(row)

                return inner

            lax.fori_loop(0, 2, block_body, 0)

            for sign in range(2):
                row, valid = rows_at(distance - 1, sign)

                @pl.when(valid)
                def _():
                    pass_on(projection_relay, row, distance - 1)

        return carry

    lax.fori_loop(0, lines + 1, step_body, 0)

    def core_copy(step):
        return remote(
            projection.at[:, dp], projection.at[:, dp], o_core_send.at[step], o_core_recv.at[step],
            dp=lax.rem(dp + step, n_dp),
        )


    def update_copy(which, target):
        rows = pl.ds(pl.multiple_of(target * hidden_rows, hidden_rows), hidden_rows)
        return remote(
            update_stage.at[which, rows], update_land.at[which, me],
            u_send.at[which, target], u_recv.at[which, me], ctx=target,
        )

    @pl.when(owner)
    def _():
        def matrix_body(which, carry):
            update_stage[which] = orthogonalize(gradient[which]).astype(jnp.bfloat16)
            for step in range(1, n_ctx):
                update_copy(which, peer(step)).start()
            return carry

        lax.fori_loop(0, 3, matrix_body, 0)
        update_land[:, me] = update_stage[:, my_rows]

    for row in range(lines):
        pair_arrived(projection_relay, row)
    for step in range(1, n_dp):
        core_copy(step).start()

    for head in range(heads):
        @pl.when(me != head)
        def _():
            remote(
                out_stage.at[0], out_land.at[head], h_send.at[0], h_recv.at[head], ctx=head
            ).wait_recv()

    for step in range(1, n_dp):
        source = lax.rem(dp + n_dp - step, n_dp)
        remote(
            projection.at[:, source], projection.at[:, source],
            o_core_send.at[step], o_core_recv.at[step], dp=source,
        ).wait()
    head_out = jnp.concatenate([out_land[head] for head in range(heads)], axis=1)
    full_out = projection[...].reshape(heads * head_dim, projection.shape[3])
    branch_out = dot_nn(head_out, full_out)
    passed_out[...] = (blocks[me].astype(jnp.float32) + branch_out).astype(jnp.bfloat16)

    for which in range(3):
        for head in range(heads):
            @pl.when(me != head)
            def _():
                remote(
                    update_stage.at[which, pl.ds(0, hidden_rows)], update_land.at[which, head],
                    u_send.at[which, 0], u_recv.at[which, head], ctx=head,
                ).wait_recv()

    update_out[...] = update_land[:, :heads]

    @pl.when(to_sec)
    def _():
        y_copy().wait_send()

    for step in range(1, n_ctx):
        target = peer(step)

        @pl.when(target < heads)
        def _():
            w_copy(target).wait_send()
            f_copy(target).wait_send()

        @pl.when(owner)
        def _():
            out_copy(target).wait_send()
            for which in range(3):
                update_copy(which, target).wait_send()

    relay_sent(input_relay)
    relay_sent(projection_relay)


def local(fresh_input, carried, qkv_weight, out_weight, rate_weight, fast_state):
    n_ctx, n_sec, n_dp = (lax.axis_size(axis) for axis in ("ctx", "sec", "dp"))
    heads = rate_weight.shape[2]
    head_dim = fast_state.shape[5]
    hidden_rows = fast_state.shape[4]
    depth = rate_weight.shape[1]
    count, width = fresh_input.shape[1:]
    assert heads <= n_ctx and n_ctx % PAIR == 0
    previous = fast_state[0, 0]

    columns = qkv_weight[0].reshape(depth, 3, heads, head_dim).transpose(2, 0, 1, 3)
    columns = columns.reshape(heads, depth, 3 * head_dim)
    rate_columns = jnp.pad(rate_weight[0].T[:, :, None], ((0, 0), (0, 0), (0, LANES - 1)))
    columns = jnp.concatenate([columns, rate_columns], axis=2)
    fast_rows = previous.astype(jnp.bfloat16)

    half = jnp.bfloat16
    dma = pltpu.SemaphoreType.DMA
    lines = n_ctx // PAIR
    any_spec = pl.BlockSpec(memory_space=pl.ANY)
    vmem_spec = pl.BlockSpec(memory_space=pltpu.VMEM)
    tokens = n_ctx * count
    hidden_all = n_ctx * hidden_rows
    flops = 2 * tokens * head_dim * (3 * width + 9 * hidden_all)
    passed, update = pl.pallas_call(
        functools.partial(kernel, (n_ctx, n_sec, n_dp, heads)),
        out_shape=[
            jax.ShapeDtypeStruct((count, width), half),
            jax.ShapeDtypeStruct((3, heads, hidden_rows, head_dim), half),
        ],
        in_specs=[any_spec] * 5,
        out_specs=[vmem_spec] * 2,
        scratch_shapes=[
            pltpu.VMEM((n_ctx, count, width), half),
            pltpu.VMEM((n_ctx, n_dp, depth, 3 * head_dim + LANES), half),
            pltpu.VMEM((3, hidden_all, head_dim), half),
            pltpu.VMEM((3, hidden_all, head_dim), jnp.float32),
            pltpu.VMEM((n_ctx, count, head_dim), half),
            pltpu.VMEM((n_ctx, count, head_dim), half),
            pltpu.VMEM((3, hidden_all, head_dim), half),
            pltpu.VMEM((3, n_ctx, hidden_rows, head_dim), half),
            pltpu.VMEM((n_ctx, n_dp, depth, width), half),
            dma((2,)), dma, dma((2,)),
            dma((n_ctx,)), dma((n_ctx,)), dma((n_ctx,)), dma((n_ctx,)),
            dma((n_dp,)), dma((n_dp,)),
            dma((lines,)), dma((lines,)), dma((lines,)), dma((lines,)), dma((lines,)),
            dma((n_ctx,)), dma((n_ctx,)), dma((3, n_ctx)), dma((3, n_ctx)),
            dma, dma((lines,)), dma((lines,)), dma((lines,)), dma((lines,)), dma((lines,)),
            dma((n_dp,)), dma((n_dp,)),
        ],
        compiler_params=pltpu.CompilerParams(
            collective_id=0, has_side_effects=True, vmem_limit_bytes=VMEM_BYTES
        ),
        cost_estimate=pl.CostEstimate(
            flops=flops, bytes_accessed=tokens * width * 2, transcendentals=4 * tokens * hidden_all
        ),
    )(fresh_input, carried, columns, fast_rows, out_weight)

    stepped = previous - update_scale * update.astype(jnp.float32)
    rescale = jnp.sqrt(jnp.mean(previous * previous, axis=-1, keepdims=True) + 1e-06) * lax.rsqrt(
        jnp.mean(stepped * stepped, axis=-1, keepdims=True) + 1e-06
    )
    new_state = (stepped * rescale)[None, None]
    return (passed[None, None], new_state)


def solution(mesh):
    in_specs = (
        P("dp", "ctx", None),
        P("sec", "dp", "ctx", None),
        P("sec", ("ctx", "dp"), None),
        P("sec", ("ctx", "dp"), None),
        P("sec", ("ctx", "dp"), None),
        P("sec", "dp", None, None, "ctx", None),
    )
    out_specs = (P("sec", "dp", "ctx", None), P("sec", "dp", None, None, "ctx", None))
    return jax.shard_map(local, mesh=mesh, in_specs=in_specs, out_specs=out_specs, check_vma=False)
```

```python
import functools

import jax
import jax.numpy as jnp
from jax import lax
from jax.experimental import pallas as pl
from jax.experimental.pallas import tpu as pltpu
from jax.sharding import PartitionSpec as P

NS_STEPS = 2
LANES = 128
PAIR = 2
VMEM_BYTES = 56 * 2**20

linear_coef = 3.4445
cubic_coef = -4.775
quintic_coef = 2.0315
update_scale = 8.0
MESH = pl.DeviceIdType.MESH


def swish(values):
    return values * jax.nn.sigmoid(values)


def unit_rows(values):
    return values * lax.rsqrt(jnp.sum(values * values, axis=-1, keepdims=True) + 1e-06)


def dot_nn(a, b):
    return jnp.dot(a, b, preferred_element_type=jnp.float32)


def dot_nt(a, b):
    return lax.dot_general(a, b, (((1,), (1,)), ((), ())), preferred_element_type=jnp.float32)


def dot_tn(a, b):
    return lax.dot_general(a, b, (((0,), (0,)), ((), ())), preferred_element_type=jnp.float32)


def parts_of(values):
    high = values.astype(jnp.bfloat16)
    return high, (values - high.astype(jnp.float32)).astype(jnp.bfloat16)


def dot_split(dot, a, b):
    return dot(a[0], b[0]) + (dot(a[0], b[1]) + dot(a[1], b[0]))


def orthogonalize(gradient):
    gradient_parts = parts_of(gradient)
    square = dot_split(dot_tn, gradient_parts, gradient_parts)
    rows = lax.broadcasted_iota(jnp.int32, square.shape, 0)
    columns = lax.broadcasted_iota(jnp.int32, square.shape, 1)
    eye = (rows == columns).astype(jnp.float32)
    trace = jnp.sum(jnp.sum(square * eye, axis=1, keepdims=True), axis=0, keepdims=True)
    inverse_norm = lax.rsqrt(trace + 1e-06)
    square = square * inverse_norm * inverse_norm
    total = None
    for iteration in range(NS_STEPS):
        square_parts = parts_of(square)
        quad = dot_split(dot_nn, square_parts, square_parts)
        poly = linear_coef * eye + cubic_coef * square + quintic_coef * quad
        poly_parts = parts_of(poly)
        if total is None:
            total = poly
        else:
            total = dot_split(dot_nn, parts_of(total), poly_parts)
        if iteration + 1 < NS_STEPS:
            left = dot_split(dot_nn, poly_parts, square_parts)
            square = dot_split(dot_nn, parts_of(left), poly_parts)
    return dot_split(dot_nn, gradient_parts, parts_of(total * inverse_norm))


def block_terms(inputs, weight_ref, fast_ref, gradient_ref):
    head_dim = fast_ref.shape[2]
    weight = weight_ref[...].reshape(inputs.shape[1], weight_ref.shape[3])
    projected = dot_nn(inputs, weight)
    query_rows = unit_rows(swish(projected[:, :head_dim])).astype(jnp.bfloat16)
    key_rows = unit_rows(swish(projected[:, head_dim : 2 * head_dim])).astype(jnp.bfloat16)
    value_rows = projected[:, 2 * head_dim : 3 * head_dim].astype(jnp.bfloat16)
    rates = jax.nn.softplus(projected[:, 3 * head_dim : 3 * head_dim + 1])
    scaled_values = (rates * value_rows.astype(jnp.float32)).astype(jnp.bfloat16)

    gate_query = dot_nt(query_rows, fast_ref[0])
    up_query = dot_nt(query_rows, fast_ref[1])
    hidden = (swish(gate_query) * up_query).astype(jnp.bfloat16)
    mixture = dot_nn(hidden, fast_ref[2])
    head_out = mixture * lax.rsqrt(jnp.mean(mixture * mixture, axis=-1, keepdims=True) + 1e-05)

    gate_pre = dot_nt(key_rows, fast_ref[0])
    up_pre = dot_nt(key_rows, fast_ref[1])
    sigma = jax.nn.sigmoid(gate_pre)
    gate_act = gate_pre * sigma
    key_hidden = (gate_act * up_pre).astype(jnp.bfloat16)
    hidden_grad = -dot_nt(scaled_values, fast_ref[2])
    up_grad = (hidden_grad * gate_act).astype(jnp.bfloat16)
    gate_grad = (hidden_grad * up_pre * sigma * (1.0 + gate_pre * (1.0 - sigma))).astype(
        jnp.bfloat16
    )
    gradient_ref[0] += dot_tn(gate_grad, key_rows)
    gradient_ref[1] += dot_tn(up_grad, key_rows)
    gradient_ref[2] -= dot_tn(key_hidden, scaled_values)
    return head_out.astype(jnp.bfloat16)


def kernel(
    sizes, fresh, carried, columns, fast_rows, out_rows, passed_out, update_out,
    blocks, weight, fast, gradient, out_stage, out_land, update_stage, update_land, projection,
    y_sem, load_sem, own_sem, w_send, w_recv, f_send, f_recv, d_send, d_recv,
    up_send, down_send, line_recv, pair_send, pair_recv, h_send, h_recv, u_send, u_recv,
    o_load, o_up_send, o_down_send, o_line_recv, o_pair_send, o_pair_recv, o_core_send, o_core_recv,
):
    n_ctx, n_sec, n_dp, heads = sizes
    lines = n_ctx // PAIR
    me = lax.axis_index("ctx")
    sec = lax.axis_index("sec")
    dp = lax.axis_index("dp")
    line, side = me // PAIR, lax.rem(me, PAIR)
    hidden_rows = fast_rows.shape[2]
    head_dim = fast_rows.shape[3]
    owner = me < heads
    from_sec = sec > 0
    to_sec = sec + 1 < n_sec

    def remote(src, dst, send, recv, **device):
        return pltpu.make_async_remote_copy(
            src_ref=src, dst_ref=dst, send_sem=send, recv_sem=recv,
            device_id=device, device_id_type=MESH,
        )

    def peer(step):
        return lax.rem(me + step, n_ctx)

    barrier = pltpu.get_barrier_semaphore()
    for step in range(1, n_ctx):
        pl.semaphore_signal(barrier, inc=1, device_id={"ctx": peer(step)}, device_id_type=MESH)
    for step in range(1, n_dp):
        pl.semaphore_signal(
            barrier, inc=1, device_id={"dp": lax.rem(dp + step, n_dp)}, device_id_type=MESH
        )

    for step in range(1, n_sec):
        pl.semaphore_signal(
            barrier, inc=1, device_id={"sec": lax.rem(sec + step, n_sec)}, device_id_type=MESH
        )
    pl.semaphore_wait(barrier, n_ctx + n_dp + n_sec - 3)

    def y_copy():
        return remote(
            carried.at[0, 0], blocks.at[me], y_sem.at[0], y_sem.at[1], sec=lax.rem(sec + 1, n_sec)
        )

    def fresh_copy():
        return pltpu.make_async_copy(fresh.at[0], blocks.at[me], load_sem)

    @pl.when(to_sec)
    def _():
        y_copy().start()

    @pl.when(sec == 0)
    def _():
        fresh_copy().start()

    my_rows = pl.ds(pl.multiple_of(me * hidden_rows, hidden_rows), hidden_rows)

    def w_copy(target):
        return remote(
            columns.at[target], weight.at[me, dp], w_send.at[target], w_recv.at[me], ctx=target
        )

    def f_copy(target):
        return remote(
            fast_rows.at[:, target], fast.at[:, my_rows], f_send.at[target], f_recv.at[me],
            ctx=target,
        )

    def own_copies():
        return (
            pltpu.make_async_copy(columns.at[me], weight.at[me, dp], own_sem.at[0]),
            pltpu.make_async_copy(fast_rows.at[:, me], fast.at[:, my_rows], own_sem.at[1]),
        )

    for step in range(1, n_ctx):
        target = peer(step)

        @pl.when(target < heads)
        def _():
            w_copy(target).start()

    for step in range(1, n_ctx):
        target = peer(step)

        @pl.when(target < heads)
        def _():
            f_copy(target).start()

    def own_projection():
        return pltpu.make_async_copy(out_rows.at[0], projection.at[me, dp], o_load)

    own_projection().start()

    @pl.when(owner)
    def _():
        for copy in own_copies():
            copy.start()
        gradient[...] = jnp.zeros_like(gradient)

    def shard(row, which):
        return row * PAIR + which

    def input_slot(at):
        return blocks.at[at]

    def projection_slot(at):
        return projection.at[at, dp]

    input_relay = (input_slot, up_send, down_send, line_recv, pair_send, pair_recv)
    projection_relay = (
        projection_slot, o_up_send, o_down_send, o_line_recv, o_pair_send, o_pair_recv
    )

    def up_copy(relay, row):
        slot = relay[0](shard(row, side))
        to = shard(lax.rem(line + 1, lines), side)
        return remote(slot, slot, relay[1].at[row], relay[3].at[row], ctx=to)

    def down_copy(relay, row):
        slot = relay[0](shard(row, side))
        to = shard(lax.rem(line + lines - 1, lines), side)
        return remote(slot, slot, relay[2].at[row], relay[3].at[row], ctx=to)

    def pair_copy(relay, row):
        slot = relay[0](shard(row, side))
        to = shard(line, 1 - side)
        return remote(slot, slot, relay[4].at[row], relay[5].at[row], ctx=to)

    def pair_arrived(relay, row):
        slot = relay[0](shard(row, 1 - side))
        to = shard(line, 1 - side)
        remote(slot, slot, relay[4].at[row], relay[5].at[row], ctx=to).wait_recv()

    def pass_on(relay, row, distance):
        @pl.when(distance > 0)
        def _():
            up_copy(relay, row).wait_recv()

        @pl.when((row <= line) & (line + 1 < lines))
        def _():
            up_copy(relay, row).start()

        @pl.when((row >= line) & (line > 0))
        def _():
            down_copy(relay, row).start()

        pair_copy(relay, row).start()

    def relay_sent(relay):
        for row in range(lines):
            @pl.when((row <= line) & (line + 1 < lines))
            def _():
                up_copy(relay, row).wait_send()

            @pl.when((row >= line) & (line > 0))
            def _():
                down_copy(relay, row).wait_send()

            pair_copy(relay, row).wait_send()

    def out_copy(at):
        return remote(
            out_stage.at[at], out_land.at[me], h_send.at[at], h_recv.at[me], ctx=at
        )

    def compute(row):
        first = row * PAIR
        tokens = blocks[pl.ds(first, PAIR)].reshape(PAIR * blocks.shape[1], blocks.shape[2])
        out = block_terms(tokens, weight, fast, gradient)
        for which in range(PAIR):
            at = first + which
            part = out[which * blocks.shape[1] : (which + 1) * blocks.shape[1]]

            @pl.when(at == me)
            def _():
                out_land[me] = part

            @pl.when(at != me)
            def _():
                out_stage[at] = part
                out_copy(at).start()

    def rows_at(distance, sign):
        row = line + distance * (1 - 2 * sign)
        valid = (row >= 0) & (row < lines) & ((distance > 0) | (sign == 0))
        return row, valid

    @pl.when(sec == 0)
    def _():
        fresh_copy().wait()

    @pl.when(from_sec)
    def _():
        y_copy().wait_recv()

    def weights_ready():
        @pl.when(owner)
        def _():
            for step in range(1, n_ctx):
                source = peer(step)
                remote(
                    columns.at[0], weight.at[source, dp], w_send.at[0], w_recv.at[source],
                    ctx=source,
                ).wait_recv()
            for copy in own_copies():
                copy.wait()
            for step in range(1, n_dp):
                remote(
                    weight.at[:, dp], weight.at[:, dp], d_send.at[step], d_recv.at[step],
                    dp=lax.rem(dp + step, n_dp),
                ).start()
            for step in range(1, n_ctx):
                source = peer(step)
                rows = pl.ds(pl.multiple_of(source * hidden_rows, hidden_rows), hidden_rows)
                remote(
                    fast_rows.at[:, 0], fast.at[:, rows], f_send.at[0], f_recv.at[source],
                    ctx=source,
                ).wait_recv()
            for step in range(1, n_dp):
                source = lax.rem(dp + n_dp - step, n_dp)
                remote(
                    weight.at[:, source], weight.at[:, source], d_send.at[step], d_recv.at[step],
                    dp=source,
                ).wait()

    def step_body(distance, carry):
        @pl.when(distance < lines)
        def _():
            for sign in range(2):
                row, valid = rows_at(distance, sign)

                @pl.when(valid)
                def _():
                    pass_on(input_relay, row, distance)

        @pl.when(distance == 1)
        def _():
            weights_ready()

        @pl.when(distance == lines - 1)
        def _():
            own_projection().wait()
            pass_on(projection_relay, line, 0)

        @pl.when(distance > 0)
        def _():
            def block_body(sign, inner):
                row, valid = rows_at(distance - 1, sign)

                @pl.when(valid)
                def _():
                    pair_arrived(input_relay, row)

                    @pl.when(owner)
                    def _():
                        compute(row)

                return inner

            lax.fori_loop(0, 2, block_body, 0)

        return carry

    lax.fori_loop(0, lines + 1, step_body, 0)

    def projection_step(distance):
        for sign in range(2):
            row, valid = rows_at(distance, sign)

            @pl.when(valid)
            def _():
                pass_on(projection_relay, row, distance)

    def core_copy(step):
        return remote(
            projection.at[:, dp], projection.at[:, dp], o_core_send.at[step], o_core_recv.at[step],
            dp=lax.rem(dp + step, n_dp),
        )


    def update_copy(which, target):
        rows = pl.ds(pl.multiple_of(target * hidden_rows, hidden_rows), hidden_rows)
        return remote(
            update_stage.at[which, rows], update_land.at[which, me],
            u_send.at[which, target], u_recv.at[which, me], ctx=target,
        )

    def matrix_body(which, carry):
        projection_step(which + 1)

        @pl.when(owner)
        def _():
            update_stage[which] = orthogonalize(gradient[which]).astype(jnp.bfloat16)
            for step in range(1, n_ctx):
                update_copy(which, peer(step)).start()

        return carry

    def rest_body(distance, carry):
        projection_step(distance)
        return carry

    lax.fori_loop(0, 3, matrix_body, 0)
    lax.fori_loop(4, max(lines, 4), rest_body, 0)

    @pl.when(owner)
    def _():
        update_land[:, me] = update_stage[:, my_rows]

    for row in range(lines):
        pair_arrived(projection_relay, row)
    for step in range(1, n_dp):
        core_copy(step).start()

    for head in range(heads):
        @pl.when(me != head)
        def _():
            remote(
                out_stage.at[0], out_land.at[head], h_send.at[0], h_recv.at[head], ctx=head
            ).wait_recv()

    for step in range(1, n_dp):
        source = lax.rem(dp + n_dp - step, n_dp)
        remote(
            projection.at[:, source], projection.at[:, source],
            o_core_send.at[step], o_core_recv.at[step], dp=source,
        ).wait()
    head_out = jnp.concatenate([out_land[head] for head in range(heads)], axis=1)
    full_out = projection[...].reshape(heads * head_dim, projection.shape[3])
    branch_out = dot_nn(head_out, full_out)
    passed_out[...] = (blocks[me].astype(jnp.float32) + branch_out).astype(jnp.bfloat16)

    for which in range(3):
        for head in range(heads):
            @pl.when(me != head)
            def _():
                remote(
                    update_stage.at[which, pl.ds(0, hidden_rows)], update_land.at[which, head],
                    u_send.at[which, 0], u_recv.at[which, head], ctx=head,
                ).wait_recv()

    update_out[...] = update_land[:, :heads]

    @pl.when(to_sec)
    def _():
        y_copy().wait_send()

    for step in range(1, n_ctx):
        target = peer(step)

        @pl.when(target < heads)
        def _():
            w_copy(target).wait_send()
            f_copy(target).wait_send()

        @pl.when(owner)
        def _():
            out_copy(target).wait_send()
            for which in range(3):
                update_copy(which, target).wait_send()

    relay_sent(input_relay)
    relay_sent(projection_relay)


def local(fresh_input, carried, qkv_weight, out_weight, rate_weight, fast_state):
    n_ctx, n_sec, n_dp = (lax.axis_size(axis) for axis in ("ctx", "sec", "dp"))
    heads = rate_weight.shape[2]
    head_dim = fast_state.shape[5]
    hidden_rows = fast_state.shape[4]
    depth = rate_weight.shape[1]
    count, width = fresh_input.shape[1:]
    assert heads <= n_ctx and n_ctx % PAIR == 0
    previous = fast_state[0, 0]

    columns = qkv_weight[0].reshape(depth, 3, heads, head_dim).transpose(2, 0, 1, 3)
    columns = columns.reshape(heads, depth, 3 * head_dim)
    rate_columns = jnp.pad(rate_weight[0].T[:, :, None], ((0, 0), (0, 0), (0, LANES - 1)))
    columns = jnp.concatenate([columns, rate_columns], axis=2)
    fast_rows = previous.astype(jnp.bfloat16)

    half = jnp.bfloat16
    dma = pltpu.SemaphoreType.DMA
    lines = n_ctx // PAIR
    any_spec = pl.BlockSpec(memory_space=pl.ANY)
    vmem_spec = pl.BlockSpec(memory_space=pltpu.VMEM)
    tokens = n_ctx * count
    hidden_all = n_ctx * hidden_rows
    flops = 2 * tokens * head_dim * (3 * width + 9 * hidden_all)
    passed, update = pl.pallas_call(
        functools.partial(kernel, (n_ctx, n_sec, n_dp, heads)),
        out_shape=[
            jax.ShapeDtypeStruct((count, width), half),
            jax.ShapeDtypeStruct((3, heads, hidden_rows, head_dim), half),
        ],
        in_specs=[any_spec] * 5,
        out_specs=[vmem_spec] * 2,
        scratch_shapes=[
            pltpu.VMEM((n_ctx, count, width), half),
            pltpu.VMEM((n_ctx, n_dp, depth, 3 * head_dim + LANES), half),
            pltpu.VMEM((3, hidden_all, head_dim), half),
            pltpu.VMEM((3, hidden_all, head_dim), jnp.float32),
            pltpu.VMEM((n_ctx, count, head_dim), half),
            pltpu.VMEM((n_ctx, count, head_dim), half),
            pltpu.VMEM((3, hidden_all, head_dim), half),
            pltpu.VMEM((3, n_ctx, hidden_rows, head_dim), half),
            pltpu.VMEM((n_ctx, n_dp, depth, width), half),
            dma((2,)), dma, dma((2,)),
            dma((n_ctx,)), dma((n_ctx,)), dma((n_ctx,)), dma((n_ctx,)),
            dma((n_dp,)), dma((n_dp,)),
            dma((lines,)), dma((lines,)), dma((lines,)), dma((lines,)), dma((lines,)),
            dma((n_ctx,)), dma((n_ctx,)), dma((3, n_ctx)), dma((3, n_ctx)),
            dma, dma((lines,)), dma((lines,)), dma((lines,)), dma((lines,)), dma((lines,)),
            dma((n_dp,)), dma((n_dp,)),
        ],
        compiler_params=pltpu.CompilerParams(
            collective_id=0, has_side_effects=True, vmem_limit_bytes=VMEM_BYTES
        ),
        cost_estimate=pl.CostEstimate(
            flops=flops, bytes_accessed=tokens * width * 2, transcendentals=4 * tokens * hidden_all
        ),
    )(fresh_input, carried, columns, fast_rows, out_weight)

    stepped = previous - update_scale * update.astype(jnp.float32)
    rescale = jnp.sqrt(jnp.mean(previous * previous, axis=-1, keepdims=True) + 1e-06) * lax.rsqrt(
        jnp.mean(stepped * stepped, axis=-1, keepdims=True) + 1e-06
    )
    new_state = (stepped * rescale)[None, None]
    return (passed[None, None], new_state)


def solution(mesh):
    in_specs = (
        P("dp", "ctx", None),
        P("sec", "dp", "ctx", None),
        P("sec", ("ctx", "dp"), None),
        P("sec", ("ctx", "dp"), None),
        P("sec", ("ctx", "dp"), None),
        P("sec", "dp", None, None, "ctx", None),
    )
    out_specs = (P("sec", "dp", "ctx", None), P("sec", "dp", None, None, "ctx", None))
    return jax.shard_map(local, mesh=mesh, in_specs=in_specs, out_specs=out_specs, check_vma=False)
```

```python
import functools

import jax
import jax.numpy as jnp
from jax import lax
from jax.experimental import pallas as pl
from jax.experimental.pallas import tpu as pltpu
from jax.sharding import PartitionSpec as P

NS_STEPS = 2
LANES = 128
PAIR = 2
CHUNKS = 2
VMEM_BYTES = 56 * 2**20

linear_coef = 3.4445
cubic_coef = -4.775
quintic_coef = 2.0315
update_scale = 8.0
MESH = pl.DeviceIdType.MESH


def swish(values):
    return values * jax.nn.sigmoid(values)


def unit_rows(values):
    return values * lax.rsqrt(jnp.sum(values * values, axis=-1, keepdims=True) + 1e-06)


def dot_nn(a, b):
    return jnp.dot(a, b, preferred_element_type=jnp.float32)


def dot_nt(a, b):
    return lax.dot_general(a, b, (((1,), (1,)), ((), ())), preferred_element_type=jnp.float32)


def dot_tn(a, b):
    return lax.dot_general(a, b, (((0,), (0,)), ((), ())), preferred_element_type=jnp.float32)


def parts_of(values):
    high = values.astype(jnp.bfloat16)
    return high, (values - high.astype(jnp.float32)).astype(jnp.bfloat16)


def dot_split(dot, a, b):
    return dot(a[0], b[0]) + (dot(a[0], b[1]) + dot(a[1], b[0]))


def orthogonalize(gradient):
    gradient_parts = parts_of(gradient)
    square = dot_split(dot_tn, gradient_parts, gradient_parts)
    rows = lax.broadcasted_iota(jnp.int32, square.shape, 0)
    columns = lax.broadcasted_iota(jnp.int32, square.shape, 1)
    eye = (rows == columns).astype(jnp.float32)
    trace = jnp.sum(jnp.sum(square * eye, axis=1, keepdims=True), axis=0, keepdims=True)
    inverse_norm = lax.rsqrt(trace + 1e-06)
    square = square * inverse_norm * inverse_norm
    total = None
    for iteration in range(NS_STEPS):
        square_parts = parts_of(square)
        quad = dot_split(dot_nn, square_parts, square_parts)
        poly = linear_coef * eye + cubic_coef * square + quintic_coef * quad
        poly_parts = parts_of(poly)
        if total is None:
            total = poly
        else:
            total = dot_split(dot_nn, parts_of(total), poly_parts)
        if iteration + 1 < NS_STEPS:
            left = dot_split(dot_nn, poly_parts, square_parts)
            square = dot_split(dot_nn, parts_of(left), poly_parts)
    return dot_split(dot_nn, gradient_parts, parts_of(total * inverse_norm))


def block_terms(inputs, weight_ref, fast_ref, gradient_ref):
    head_dim = fast_ref.shape[2]
    weight = weight_ref[...].reshape(inputs.shape[1], weight_ref.shape[3])
    projected = dot_nn(inputs, weight)
    query_rows = unit_rows(swish(projected[:, :head_dim])).astype(jnp.bfloat16)
    key_rows = unit_rows(swish(projected[:, head_dim : 2 * head_dim])).astype(jnp.bfloat16)
    value_rows = projected[:, 2 * head_dim : 3 * head_dim].astype(jnp.bfloat16)
    rates = jax.nn.softplus(projected[:, 3 * head_dim : 3 * head_dim + 1])
    scaled_values = (rates * value_rows.astype(jnp.float32)).astype(jnp.bfloat16)

    gate_query = dot_nt(query_rows, fast_ref[0])
    up_query = dot_nt(query_rows, fast_ref[1])
    hidden = (swish(gate_query) * up_query).astype(jnp.bfloat16)
    mixture = dot_nn(hidden, fast_ref[2])
    head_out = mixture * lax.rsqrt(jnp.mean(mixture * mixture, axis=-1, keepdims=True) + 1e-05)

    gate_pre = dot_nt(key_rows, fast_ref[0])
    up_pre = dot_nt(key_rows, fast_ref[1])
    sigma = jax.nn.sigmoid(gate_pre)
    gate_act = gate_pre * sigma
    key_hidden = (gate_act * up_pre).astype(jnp.bfloat16)
    hidden_grad = -dot_nt(scaled_values, fast_ref[2])
    up_grad = (hidden_grad * gate_act).astype(jnp.bfloat16)
    gate_grad = (hidden_grad * up_pre * sigma * (1.0 + gate_pre * (1.0 - sigma))).astype(
        jnp.bfloat16
    )
    gradient_ref[0] += dot_tn(gate_grad, key_rows)
    gradient_ref[1] += dot_tn(up_grad, key_rows)
    gradient_ref[2] -= dot_tn(key_hidden, scaled_values)
    return head_out.astype(jnp.bfloat16)


def kernel(
    sizes, fresh, carried, columns, fast_rows, out_rows, passed_out, update_out,
    blocks, weight, fast, gradient, out_stage, out_land, update_stage, update_land, projection,
    y_sem, load_sem, own_sem, w_send, w_recv, f_send, f_recv, d_send, d_recv,
    up_send, down_send, line_recv, pair_send, pair_recv, h_send, h_recv, u_send, u_recv,
    o_load, o_up_send, o_down_send, o_line_recv, o_pair_send, o_pair_recv, o_core_send, o_core_recv,
):
    n_ctx, n_sec, n_dp, heads = sizes
    lines = n_ctx // PAIR
    me = lax.axis_index("ctx")
    sec = lax.axis_index("sec")
    dp = lax.axis_index("dp")
    line, side = me // PAIR, lax.rem(me, PAIR)
    hidden_rows = fast_rows.shape[2]
    head_dim = fast_rows.shape[3]
    owner = me < heads
    from_sec = sec > 0
    to_sec = sec + 1 < n_sec

    def remote(src, dst, send, recv, **device):
        return pltpu.make_async_remote_copy(
            src_ref=src, dst_ref=dst, send_sem=send, recv_sem=recv,
            device_id=device, device_id_type=MESH,
        )

    def peer(step):
        return lax.rem(me + step, n_ctx)

    barrier = pltpu.get_barrier_semaphore()
    for step in range(1, n_ctx):
        pl.semaphore_signal(barrier, inc=1, device_id={"ctx": peer(step)}, device_id_type=MESH)
    for step in range(1, n_dp):
        pl.semaphore_signal(
            barrier, inc=1, device_id={"dp": lax.rem(dp + step, n_dp)}, device_id_type=MESH
        )

    for step in range(1, n_sec):
        pl.semaphore_signal(
            barrier, inc=1, device_id={"sec": lax.rem(sec + step, n_sec)}, device_id_type=MESH
        )
    pl.semaphore_wait(barrier, n_ctx + n_dp + n_sec - 3)

    part = blocks.shape[1] // CHUNKS

    def y_copy(chunk):
        rows = pl.ds(chunk * part, part)
        return remote(
            carried.at[0, 0, rows], blocks.at[me, rows], y_sem.at[0, chunk], y_sem.at[1, chunk],
            sec=lax.rem(sec + 1, n_sec),
        )

    def fresh_copy():
        return pltpu.make_async_copy(fresh.at[0], blocks.at[me], load_sem)

    @pl.when(to_sec)
    def _():
        for chunk in range(CHUNKS):
            y_copy(chunk).start()

    @pl.when(sec == 0)
    def _():
        fresh_copy().start()

    my_rows = pl.ds(pl.multiple_of(me * hidden_rows, hidden_rows), hidden_rows)

    def w_copy(target):
        return remote(
            columns.at[target], weight.at[me, dp], w_send.at[target], w_recv.at[me], ctx=target
        )

    def f_copy(target):
        return remote(
            fast_rows.at[:, target], fast.at[:, my_rows], f_send.at[target], f_recv.at[me],
            ctx=target,
        )

    def own_copies():
        return (
            pltpu.make_async_copy(columns.at[me], weight.at[me, dp], own_sem.at[0]),
            pltpu.make_async_copy(fast_rows.at[:, me], fast.at[:, my_rows], own_sem.at[1]),
        )

    for step in range(1, n_ctx):
        target = peer(step)

        @pl.when(target < heads)
        def _():
            w_copy(target).start()

    for step in range(1, n_ctx):
        target = peer(step)

        @pl.when(target < heads)
        def _():
            f_copy(target).start()

    def own_projection():
        return pltpu.make_async_copy(out_rows.at[0], projection.at[me, dp], o_load)

    own_projection().start()

    @pl.when(owner)
    def _():
        for copy in own_copies():
            copy.start()
        gradient[...] = jnp.zeros_like(gradient)

    def shard(row, which):
        return row * PAIR + which

    def input_relay(chunk):
        def slot(at):
            return blocks.at[at, pl.ds(chunk * part, part)]

        sems = (up_send, down_send, line_recv, pair_send, pair_recv)
        return (slot,) + tuple(sem.at[chunk] for sem in sems)

    input_relays = [input_relay(chunk) for chunk in range(CHUNKS)]

    def projection_slot(at):
        return projection.at[at, dp]

    projection_relay = (
        projection_slot, o_up_send, o_down_send, o_line_recv, o_pair_send, o_pair_recv
    )

    def up_copy(relay, row):
        slot = relay[0](shard(row, side))
        to = shard(lax.rem(line + 1, lines), side)
        return remote(slot, slot, relay[1].at[row], relay[3].at[row], ctx=to)

    def down_copy(relay, row):
        slot = relay[0](shard(row, side))
        to = shard(lax.rem(line + lines - 1, lines), side)
        return remote(slot, slot, relay[2].at[row], relay[3].at[row], ctx=to)

    def pair_copy(relay, row):
        slot = relay[0](shard(row, side))
        to = shard(line, 1 - side)
        return remote(slot, slot, relay[4].at[row], relay[5].at[row], ctx=to)

    def pair_arrived(relay, row):
        slot = relay[0](shard(row, 1 - side))
        to = shard(line, 1 - side)
        remote(slot, slot, relay[4].at[row], relay[5].at[row], ctx=to).wait_recv()

    def pass_on(relay, row, distance):
        @pl.when(distance > 0)
        def _():
            up_copy(relay, row).wait_recv()

        @pl.when((row <= line) & (line + 1 < lines))
        def _():
            up_copy(relay, row).start()

        @pl.when((row >= line) & (line > 0))
        def _():
            down_copy(relay, row).start()

        pair_copy(relay, row).start()

    def relay_sent(relay):
        for row in range(lines):
            @pl.when((row <= line) & (line + 1 < lines))
            def _():
                up_copy(relay, row).wait_send()

            @pl.when((row >= line) & (line > 0))
            def _():
                down_copy(relay, row).wait_send()

            pair_copy(relay, row).wait_send()

    def out_copy(at):
        return remote(
            out_stage.at[at], out_land.at[me], h_send.at[at], h_recv.at[me], ctx=at
        )

    def compute(row):
        first = row * PAIR
        tokens = blocks[pl.ds(first, PAIR)].reshape(PAIR * blocks.shape[1], blocks.shape[2])
        out = block_terms(tokens, weight, fast, gradient)
        for which in range(PAIR):
            at = first + which
            part = out[which * blocks.shape[1] : (which + 1) * blocks.shape[1]]

            @pl.when(at == me)
            def _():
                out_land[me] = part

            @pl.when(at != me)
            def _():
                out_stage[at] = part
                out_copy(at).start()

    def rows_at(distance, sign):
        row = line + distance * (1 - 2 * sign)
        valid = (row >= 0) & (row < lines) & ((distance > 0) | (sign == 0))
        return row, valid

    @pl.when(sec == 0)
    def _():
        fresh_copy().wait()

    def weights_ready():
        @pl.when(owner)
        def _():
            for step in range(1, n_ctx):
                source = peer(step)
                remote(
                    columns.at[0], weight.at[source, dp], w_send.at[0], w_recv.at[source],
                    ctx=source,
                ).wait_recv()
            for copy in own_copies():
                copy.wait()
            for step in range(1, n_dp):
                remote(
                    weight.at[:, dp], weight.at[:, dp], d_send.at[step], d_recv.at[step],
                    dp=lax.rem(dp + step, n_dp),
                ).start()
            for step in range(1, n_ctx):
                source = peer(step)
                rows = pl.ds(pl.multiple_of(source * hidden_rows, hidden_rows), hidden_rows)
                remote(
                    fast_rows.at[:, 0], fast.at[:, rows], f_send.at[0], f_recv.at[source],
                    ctx=source,
                ).wait_recv()
            for step in range(1, n_dp):
                source = lax.rem(dp + n_dp - step, n_dp)
                remote(
                    weight.at[:, source], weight.at[:, source], d_send.at[step], d_recv.at[step],
                    dp=source,
                ).wait()

    def step_body(distance, carry):
        @pl.when(distance < lines)
        def _():
            for chunk, relay in enumerate(input_relays):
                @pl.when(from_sec & (distance == 0))
                def _():
                    y_copy(chunk).wait_recv()

                for sign in range(2):
                    row, valid = rows_at(distance, sign)

                    @pl.when(valid)
                    def _():
                        pass_on(relay, row, distance)

        @pl.when(distance == 1)
        def _():
            weights_ready()
            own_projection().wait()

        @pl.when(distance > 0)
        def _():
            def block_body(sign, inner):
                row, valid = rows_at(distance - 1, sign)

                @pl.when(valid)
                def _():
                    for relay in input_relays:
                        pair_arrived(relay, row)

                    @pl.when(owner)
                    def _():
                        compute(row)

                return inner

            lax.fori_loop(0, 2, block_body, 0)

            for sign in range(2):
                row, valid = rows_at(distance - 1, sign)

                @pl.when(valid)
                def _():
                    pass_on(projection_relay, row, distance - 1)

        return carry

    lax.fori_loop(0, lines + 1, step_body, 0)

    def core_copy(step):
        return remote(
            projection.at[:, dp], projection.at[:, dp], o_core_send.at[step], o_core_recv.at[step],
            dp=lax.rem(dp + step, n_dp),
        )


    def update_copy(which, target):
        rows = pl.ds(pl.multiple_of(target * hidden_rows, hidden_rows), hidden_rows)
        return remote(
            update_stage.at[which, rows], update_land.at[which, me],
            u_send.at[which, target], u_recv.at[which, me], ctx=target,
        )

    @pl.when(owner)
    def _():
        def matrix_body(which, carry):
            update_stage[which] = orthogonalize(gradient[which]).astype(jnp.bfloat16)
            for step in range(1, n_ctx):
                update_copy(which, peer(step)).start()
            return carry

        lax.fori_loop(0, 3, matrix_body, 0)
        update_land[:, me] = update_stage[:, my_rows]

    for row in range(lines):
        pair_arrived(projection_relay, row)
    for step in range(1, n_dp):
        core_copy(step).start()

    for head in range(heads):
        @pl.when(me != head)
        def _():
            remote(
                out_stage.at[0], out_land.at[head], h_send.at[0], h_recv.at[head], ctx=head
            ).wait_recv()

    for step in range(1, n_dp):
        source = lax.rem(dp + n_dp - step, n_dp)
        remote(
            projection.at[:, source], projection.at[:, source],
            o_core_send.at[step], o_core_recv.at[step], dp=source,
        ).wait()
    head_out = jnp.concatenate([out_land[head] for head in range(heads)], axis=1)
    full_out = projection[...].reshape(heads * head_dim, projection.shape[3])
    branch_out = dot_nn(head_out, full_out)
    passed_out[...] = (blocks[me].astype(jnp.float32) + branch_out).astype(jnp.bfloat16)

    for which in range(3):
        for head in range(heads):
            @pl.when(me != head)
            def _():
                remote(
                    update_stage.at[which, pl.ds(0, hidden_rows)], update_land.at[which, head],
                    u_send.at[which, 0], u_recv.at[which, head], ctx=head,
                ).wait_recv()

    update_out[...] = update_land[:, :heads]

    @pl.when(to_sec)
    def _():
        for chunk in range(CHUNKS):
            y_copy(chunk).wait_send()

    for step in range(1, n_ctx):
        target = peer(step)

        @pl.when(target < heads)
        def _():
            w_copy(target).wait_send()
            f_copy(target).wait_send()

        @pl.when(owner)
        def _():
            out_copy(target).wait_send()
            for which in range(3):
                update_copy(which, target).wait_send()

    for relay in input_relays:
        relay_sent(relay)
    relay_sent(projection_relay)


def local(fresh_input, carried, qkv_weight, out_weight, rate_weight, fast_state):
    n_ctx, n_sec, n_dp = (lax.axis_size(axis) for axis in ("ctx", "sec", "dp"))
    heads = rate_weight.shape[2]
    head_dim = fast_state.shape[5]
    hidden_rows = fast_state.shape[4]
    depth = rate_weight.shape[1]
    count, width = fresh_input.shape[1:]
    assert heads <= n_ctx and n_ctx % PAIR == 0
    previous = fast_state[0, 0]

    columns = qkv_weight[0].reshape(depth, 3, heads, head_dim).transpose(2, 0, 1, 3)
    columns = columns.reshape(heads, depth, 3 * head_dim)
    rate_columns = jnp.pad(rate_weight[0].T[:, :, None], ((0, 0), (0, 0), (0, LANES - 1)))
    columns = jnp.concatenate([columns, rate_columns], axis=2)
    fast_rows = previous.astype(jnp.bfloat16)

    half = jnp.bfloat16
    dma = pltpu.SemaphoreType.DMA
    lines = n_ctx // PAIR
    any_spec = pl.BlockSpec(memory_space=pl.ANY)
    vmem_spec = pl.BlockSpec(memory_space=pltpu.VMEM)
    tokens = n_ctx * count
    hidden_all = n_ctx * hidden_rows
    flops = 2 * tokens * head_dim * (3 * width + 9 * hidden_all)
    passed, update = pl.pallas_call(
        functools.partial(kernel, (n_ctx, n_sec, n_dp, heads)),
        out_shape=[
            jax.ShapeDtypeStruct((count, width), half),
            jax.ShapeDtypeStruct((3, heads, hidden_rows, head_dim), half),
        ],
        in_specs=[any_spec] * 5,
        out_specs=[vmem_spec] * 2,
        scratch_shapes=[
            pltpu.VMEM((n_ctx, count, width), half),
            pltpu.VMEM((n_ctx, n_dp, depth, 3 * head_dim + LANES), half),
            pltpu.VMEM((3, hidden_all, head_dim), half),
            pltpu.VMEM((3, hidden_all, head_dim), jnp.float32),
            pltpu.VMEM((n_ctx, count, head_dim), half),
            pltpu.VMEM((n_ctx, count, head_dim), half),
            pltpu.VMEM((3, hidden_all, head_dim), half),
            pltpu.VMEM((3, n_ctx, hidden_rows, head_dim), half),
            pltpu.VMEM((n_ctx, n_dp, depth, width), half),
            dma((2, CHUNKS)), dma, dma((2,)),
            dma((n_ctx,)), dma((n_ctx,)), dma((n_ctx,)), dma((n_ctx,)),
            dma((n_dp,)), dma((n_dp,)),
            dma((CHUNKS, lines)), dma((CHUNKS, lines)), dma((CHUNKS, lines)),
            dma((CHUNKS, lines)), dma((CHUNKS, lines)),
            dma((n_ctx,)), dma((n_ctx,)), dma((3, n_ctx)), dma((3, n_ctx)),
            dma, dma((lines,)), dma((lines,)), dma((lines,)), dma((lines,)), dma((lines,)),
            dma((n_dp,)), dma((n_dp,)),
        ],
        compiler_params=pltpu.CompilerParams(
            collective_id=0, has_side_effects=True, vmem_limit_bytes=VMEM_BYTES
        ),
        cost_estimate=pl.CostEstimate(
            flops=flops, bytes_accessed=tokens * width * 2, transcendentals=4 * tokens * hidden_all
        ),
    )(fresh_input, carried, columns, fast_rows, out_weight)

    stepped = previous - update_scale * update.astype(jnp.float32)
    rescale = jnp.sqrt(jnp.mean(previous * previous, axis=-1, keepdims=True) + 1e-06) * lax.rsqrt(
        jnp.mean(stepped * stepped, axis=-1, keepdims=True) + 1e-06
    )
    new_state = (stepped * rescale)[None, None]
    return (passed[None, None], new_state)


def solution(mesh):
    in_specs = (
        P("dp", "ctx", None),
        P("sec", "dp", "ctx", None),
        P("sec", ("ctx", "dp"), None),
        P("sec", ("ctx", "dp"), None),
        P("sec", ("ctx", "dp"), None),
        P("sec", "dp", None, None, "ctx", None),
    )
    out_specs = (P("sec", "dp", "ctx", None), P("sec", "dp", None, None, "ctx", None))
    return jax.shard_map(local, mesh=mesh, in_specs=in_specs, out_specs=out_specs, check_vma=False)
```

```python
import functools

import jax
import jax.numpy as jnp
from jax import lax
from jax.experimental import pallas as pl
from jax.experimental.pallas import tpu as pltpu
from jax.sharding import PartitionSpec as P

NS_STEPS = 2
LANES = 128
PAIR = 2
CHUNKS = 4
VMEM_BYTES = 56 * 2**20

linear_coef = 3.4445
cubic_coef = -4.775
quintic_coef = 2.0315
update_scale = 8.0
MESH = pl.DeviceIdType.MESH


def swish(values):
    return values * jax.nn.sigmoid(values)


def unit_rows(values):
    return values * lax.rsqrt(jnp.sum(values * values, axis=-1, keepdims=True) + 1e-06)


def dot_nn(a, b):
    return jnp.dot(a, b, preferred_element_type=jnp.float32)


def dot_nt(a, b):
    return lax.dot_general(a, b, (((1,), (1,)), ((), ())), preferred_element_type=jnp.float32)


def dot_tn(a, b):
    return lax.dot_general(a, b, (((0,), (0,)), ((), ())), preferred_element_type=jnp.float32)


def parts_of(values):
    high = values.astype(jnp.bfloat16)
    return high, (values - high.astype(jnp.float32)).astype(jnp.bfloat16)


def dot_split(dot, a, b):
    return dot(a[0], b[0]) + (dot(a[0], b[1]) + dot(a[1], b[0]))


def orthogonalize(gradient):
    gradient_parts = parts_of(gradient)
    square = dot_split(dot_tn, gradient_parts, gradient_parts)
    rows = lax.broadcasted_iota(jnp.int32, square.shape, 0)
    columns = lax.broadcasted_iota(jnp.int32, square.shape, 1)
    eye = (rows == columns).astype(jnp.float32)
    trace = jnp.sum(jnp.sum(square * eye, axis=1, keepdims=True), axis=0, keepdims=True)
    inverse_norm = lax.rsqrt(trace + 1e-06)
    square = square * inverse_norm * inverse_norm
    total = None
    for iteration in range(NS_STEPS):
        square_parts = parts_of(square)
        quad = dot_split(dot_nn, square_parts, square_parts)
        poly = linear_coef * eye + cubic_coef * square + quintic_coef * quad
        poly_parts = parts_of(poly)
        if total is None:
            total = poly
        else:
            total = dot_split(dot_nn, parts_of(total), poly_parts)
        if iteration + 1 < NS_STEPS:
            left = dot_split(dot_nn, poly_parts, square_parts)
            square = dot_split(dot_nn, parts_of(left), poly_parts)
    return dot_split(dot_nn, gradient_parts, parts_of(total * inverse_norm))


def block_terms(inputs, weight_ref, fast_ref, gradient_ref):
    head_dim = fast_ref.shape[2]
    weight = weight_ref[...].reshape(inputs.shape[1], weight_ref.shape[3])
    projected = dot_nn(inputs, weight)
    query_rows = unit_rows(swish(projected[:, :head_dim])).astype(jnp.bfloat16)
    key_rows = unit_rows(swish(projected[:, head_dim : 2 * head_dim])).astype(jnp.bfloat16)
    value_rows = projected[:, 2 * head_dim : 3 * head_dim].astype(jnp.bfloat16)
    rates = jax.nn.softplus(projected[:, 3 * head_dim : 3 * head_dim + 1])
    scaled_values = (rates * value_rows.astype(jnp.float32)).astype(jnp.bfloat16)

    gate_query = dot_nt(query_rows, fast_ref[0])
    up_query = dot_nt(query_rows, fast_ref[1])
    hidden = (swish(gate_query) * up_query).astype(jnp.bfloat16)
    mixture = dot_nn(hidden, fast_ref[2])
    head_out = mixture * lax.rsqrt(jnp.mean(mixture * mixture, axis=-1, keepdims=True) + 1e-05)

    gate_pre = dot_nt(key_rows, fast_ref[0])
    up_pre = dot_nt(key_rows, fast_ref[1])
    sigma = jax.nn.sigmoid(gate_pre)
    gate_act = gate_pre * sigma
    key_hidden = (gate_act * up_pre).astype(jnp.bfloat16)
    hidden_grad = -dot_nt(scaled_values, fast_ref[2])
    up_grad = (hidden_grad * gate_act).astype(jnp.bfloat16)
    gate_grad = (hidden_grad * up_pre * sigma * (1.0 + gate_pre * (1.0 - sigma))).astype(
        jnp.bfloat16
    )
    gradient_ref[0] += dot_tn(gate_grad, key_rows)
    gradient_ref[1] += dot_tn(up_grad, key_rows)
    gradient_ref[2] -= dot_tn(key_hidden, scaled_values)
    return head_out.astype(jnp.bfloat16)


def kernel(
    sizes, fresh, carried, columns, fast_rows, out_rows, passed_out, update_out,
    blocks, weight, fast, gradient, out_stage, out_land, update_stage, update_land, projection,
    y_sem, load_sem, own_sem, w_send, w_recv, f_send, f_recv, d_send, d_recv,
    up_send, down_send, line_recv, pair_send, pair_recv, h_send, h_recv, u_send, u_recv,
    o_load, o_up_send, o_down_send, o_line_recv, o_pair_send, o_pair_recv, o_core_send, o_core_recv,
):
    n_ctx, n_sec, n_dp, heads = sizes
    lines = n_ctx // PAIR
    me = lax.axis_index("ctx")
    sec = lax.axis_index("sec")
    dp = lax.axis_index("dp")
    line, side = me // PAIR, lax.rem(me, PAIR)
    hidden_rows = fast_rows.shape[2]
    head_dim = fast_rows.shape[3]
    shift = (n_ctx - heads) // 2
    owner = (me >= shift) & (me < shift + heads)
    from_sec = sec > 0
    to_sec = sec + 1 < n_sec

    def remote(src, dst, send, recv, **device):
        return pltpu.make_async_remote_copy(
            src_ref=src, dst_ref=dst, send_sem=send, recv_sem=recv,
            device_id=device, device_id_type=MESH,
        )

    def peer(step):
        return lax.rem(me + step, n_ctx)

    barrier = pltpu.get_barrier_semaphore()
    for step in range(1, n_ctx):
        pl.semaphore_signal(barrier, inc=1, device_id={"ctx": peer(step)}, device_id_type=MESH)
    for step in range(1, n_dp):
        pl.semaphore_signal(
            barrier, inc=1, device_id={"dp": lax.rem(dp + step, n_dp)}, device_id_type=MESH
        )

    for step in range(1, n_sec):
        pl.semaphore_signal(
            barrier, inc=1, device_id={"sec": lax.rem(sec + step, n_sec)}, device_id_type=MESH
        )
    pl.semaphore_wait(barrier, n_ctx + n_dp + n_sec - 3)

    part = blocks.shape[1] // CHUNKS

    def y_copy(chunk):
        rows = pl.ds(chunk * part, part)
        return remote(
            carried.at[0, 0, rows], blocks.at[me, rows], y_sem.at[0, chunk], y_sem.at[1, chunk],
            sec=lax.rem(sec + 1, n_sec),
        )

    def fresh_copy():
        return pltpu.make_async_copy(fresh.at[0], blocks.at[me], load_sem)

    @pl.when(to_sec)
    def _():
        for chunk in range(CHUNKS):
            y_copy(chunk).start()

    @pl.when(sec == 0)
    def _():
        fresh_copy().start()

    my_rows = pl.ds(pl.multiple_of(me * hidden_rows, hidden_rows), hidden_rows)

    def w_copy(target):
        return remote(
            columns.at[target - shift], weight.at[me, dp], w_send.at[target], w_recv.at[me], ctx=target
        )

    def f_copy(target):
        return remote(
            fast_rows.at[:, target - shift], fast.at[:, my_rows], f_send.at[target], f_recv.at[me],
            ctx=target,
        )

    def own_copies():
        return (
            pltpu.make_async_copy(columns.at[me - shift], weight.at[me, dp], own_sem.at[0]),
            pltpu.make_async_copy(fast_rows.at[:, me - shift], fast.at[:, my_rows], own_sem.at[1]),
        )

    for step in range(1, n_ctx):
        target = peer(step)

        @pl.when((target >= shift) & (target < shift + heads))
        def _():
            w_copy(target).start()

    for step in range(1, n_ctx):
        target = peer(step)

        @pl.when((target >= shift) & (target < shift + heads))
        def _():
            f_copy(target).start()

    def own_projection():
        return pltpu.make_async_copy(out_rows.at[0], projection.at[me, dp], o_load)

    own_projection().start()

    @pl.when(owner)
    def _():
        for copy in own_copies():
            copy.start()
        gradient[...] = jnp.zeros_like(gradient)

    def shard(row, which):
        return row * PAIR + which

    def input_relay(chunk):
        def slot(at):
            return blocks.at[at, pl.ds(chunk * part, part)]

        sems = (up_send, down_send, line_recv, pair_send, pair_recv)
        return (slot,) + tuple(sem.at[chunk] for sem in sems)

    input_relays = [input_relay(chunk) for chunk in range(CHUNKS)]

    def projection_slot(at):
        return projection.at[at, dp]

    projection_relay = (
        projection_slot, o_up_send, o_down_send, o_line_recv, o_pair_send, o_pair_recv
    )

    def up_copy(relay, row):
        slot = relay[0](shard(row, side))
        to = shard(lax.rem(line + 1, lines), side)
        return remote(slot, slot, relay[1].at[row], relay[3].at[row], ctx=to)

    def down_copy(relay, row):
        slot = relay[0](shard(row, side))
        to = shard(lax.rem(line + lines - 1, lines), side)
        return remote(slot, slot, relay[2].at[row], relay[3].at[row], ctx=to)

    def pair_copy(relay, row):
        slot = relay[0](shard(row, side))
        to = shard(line, 1 - side)
        return remote(slot, slot, relay[4].at[row], relay[5].at[row], ctx=to)

    def pair_arrived(relay, row):
        slot = relay[0](shard(row, 1 - side))
        to = shard(line, 1 - side)
        remote(slot, slot, relay[4].at[row], relay[5].at[row], ctx=to).wait_recv()

    def pass_on(relay, row, distance):
        @pl.when(distance > 0)
        def _():
            up_copy(relay, row).wait_recv()

        @pl.when((row <= line) & (line + 1 < lines))
        def _():
            up_copy(relay, row).start()

        @pl.when((row >= line) & (line > 0))
        def _():
            down_copy(relay, row).start()

        pair_copy(relay, row).start()

    def relay_sent(relay):
        for row in range(lines):
            @pl.when((row <= line) & (line + 1 < lines))
            def _():
                up_copy(relay, row).wait_send()

            @pl.when((row >= line) & (line > 0))
            def _():
                down_copy(relay, row).wait_send()

            pair_copy(relay, row).wait_send()

    def out_copy(at):
        return remote(
            out_stage.at[at], out_land.at[me], h_send.at[at], h_recv.at[me], ctx=at
        )

    def compute(row):
        first = row * PAIR
        tokens = blocks[pl.ds(first, PAIR)].reshape(PAIR * blocks.shape[1], blocks.shape[2])
        out = block_terms(tokens, weight, fast, gradient)
        for which in range(PAIR):
            at = first + which
            part = out[which * blocks.shape[1] : (which + 1) * blocks.shape[1]]

            @pl.when(at == me)
            def _():
                out_land[me] = part

            @pl.when(at != me)
            def _():
                out_stage[at] = part
                out_copy(at).start()

    def rows_at(distance, sign):
        row = line + distance * (1 - 2 * sign)
        valid = (row >= 0) & (row < lines) & ((distance > 0) | (sign == 0))
        return row, valid

    @pl.when(sec == 0)
    def _():
        fresh_copy().wait()

    def weights_ready():
        @pl.when(owner)
        def _():
            for step in range(1, n_ctx):
                source = peer(step)
                remote(
                    columns.at[0], weight.at[source, dp], w_send.at[0], w_recv.at[source],
                    ctx=source,
                ).wait_recv()
            for copy in own_copies():
                copy.wait()
            for step in range(1, n_dp):
                remote(
                    weight.at[:, dp], weight.at[:, dp], d_send.at[step], d_recv.at[step],
                    dp=lax.rem(dp + step, n_dp),
                ).start()
            for step in range(1, n_ctx):
                source = peer(step)
                rows = pl.ds(pl.multiple_of(source * hidden_rows, hidden_rows), hidden_rows)
                remote(
                    fast_rows.at[:, 0], fast.at[:, rows], f_send.at[0], f_recv.at[source],
                    ctx=source,
                ).wait_recv()
            for step in range(1, n_dp):
                source = lax.rem(dp + n_dp - step, n_dp)
                remote(
                    weight.at[:, source], weight.at[:, source], d_send.at[step], d_recv.at[step],
                    dp=source,
                ).wait()

    def step_body(distance, carry):
        @pl.when(distance < lines)
        def _():
            for chunk, relay in enumerate(input_relays):
                @pl.when(from_sec & (distance == 0))
                def _():
                    y_copy(chunk).wait_recv()

                for sign in range(2):
                    row, valid = rows_at(distance, sign)

                    @pl.when(valid)
                    def _():
                        pass_on(relay, row, distance)

        @pl.when(distance == 1)
        def _():
            weights_ready()
            own_projection().wait()

        @pl.when(distance > 0)
        def _():
            def block_body(sign, inner):
                row, valid = rows_at(distance - 1, sign)

                @pl.when(valid)
                def _():
                    for relay in input_relays:
                        pair_arrived(relay, row)

                    @pl.when(owner)
                    def _():
                        compute(row)

                return inner

            lax.fori_loop(0, 2, block_body, 0)

            for sign in range(2):
                row, valid = rows_at(distance - 1, sign)

                @pl.when(valid)
                def _():
                    pass_on(projection_relay, row, distance - 1)

        return carry

    lax.fori_loop(0, lines + 1, step_body, 0)

    def core_copy(step):
        return remote(
            projection.at[:, dp], projection.at[:, dp], o_core_send.at[step], o_core_recv.at[step],
            dp=lax.rem(dp + step, n_dp),
        )


    def update_copy(which, target):
        rows = pl.ds(pl.multiple_of(target * hidden_rows, hidden_rows), hidden_rows)
        return remote(
            update_stage.at[which, rows], update_land.at[which, me],
            u_send.at[which, target], u_recv.at[which, me], ctx=target,
        )

    @pl.when(owner)
    def _():
        def matrix_body(which, carry):
            update_stage[which] = orthogonalize(gradient[which]).astype(jnp.bfloat16)
            for step in range(1, n_ctx):
                update_copy(which, peer(step)).start()
            return carry

        lax.fori_loop(0, 3, matrix_body, 0)
        update_land[:, me] = update_stage[:, my_rows]

    for row in range(lines):
        pair_arrived(projection_relay, row)
    for step in range(1, n_dp):
        core_copy(step).start()

    for head in range(shift, shift + heads):
        @pl.when(me != head)
        def _():
            remote(
                out_stage.at[0], out_land.at[head], h_send.at[0], h_recv.at[head], ctx=head
            ).wait_recv()

    for step in range(1, n_dp):
        source = lax.rem(dp + n_dp - step, n_dp)
        remote(
            projection.at[:, source], projection.at[:, source],
            o_core_send.at[step], o_core_recv.at[step], dp=source,
        ).wait()
    head_out = jnp.concatenate([out_land[shift + head] for head in range(heads)], axis=1)
    full_out = projection[...].reshape(heads * head_dim, projection.shape[3])
    branch_out = dot_nn(head_out, full_out)
    passed_out[...] = (blocks[me].astype(jnp.float32) + branch_out).astype(jnp.bfloat16)

    for which in range(3):
        for head in range(shift, shift + heads):
            @pl.when(me != head)
            def _():
                remote(
                    update_stage.at[which, pl.ds(0, hidden_rows)], update_land.at[which, head],
                    u_send.at[which, 0], u_recv.at[which, head], ctx=head,
                ).wait_recv()

    update_out[...] = update_land[:, shift : shift + heads]

    @pl.when(to_sec)
    def _():
        for chunk in range(CHUNKS):
            y_copy(chunk).wait_send()

    for step in range(1, n_ctx):
        target = peer(step)

        @pl.when((target >= shift) & (target < shift + heads))
        def _():
            w_copy(target).wait_send()
            f_copy(target).wait_send()

        @pl.when(owner)
        def _():
            out_copy(target).wait_send()
            for which in range(3):
                update_copy(which, target).wait_send()

    for relay in input_relays:
        relay_sent(relay)
    relay_sent(projection_relay)


def local(fresh_input, carried, qkv_weight, out_weight, rate_weight, fast_state):
    n_ctx, n_sec, n_dp = (lax.axis_size(axis) for axis in ("ctx", "sec", "dp"))
    heads = rate_weight.shape[2]
    head_dim = fast_state.shape[5]
    hidden_rows = fast_state.shape[4]
    depth = rate_weight.shape[1]
    count, width = fresh_input.shape[1:]
    assert heads <= n_ctx and n_ctx % PAIR == 0
    previous = fast_state[0, 0]

    columns = qkv_weight[0].reshape(depth, 3, heads, head_dim).transpose(2, 0, 1, 3)
    columns = columns.reshape(heads, depth, 3 * head_dim)
    rate_columns = jnp.pad(rate_weight[0].T[:, :, None], ((0, 0), (0, 0), (0, LANES - 1)))
    columns = jnp.concatenate([columns, rate_columns], axis=2)
    fast_rows = previous.astype(jnp.bfloat16)

    half = jnp.bfloat16
    dma = pltpu.SemaphoreType.DMA
    lines = n_ctx // PAIR
    any_spec = pl.BlockSpec(memory_space=pl.ANY)
    vmem_spec = pl.BlockSpec(memory_space=pltpu.VMEM)
    tokens = n_ctx * count
    hidden_all = n_ctx * hidden_rows
    flops = 2 * tokens * head_dim * (3 * width + 9 * hidden_all)
    passed, update = pl.pallas_call(
        functools.partial(kernel, (n_ctx, n_sec, n_dp, heads)),
        out_shape=[
            jax.ShapeDtypeStruct((count, width), half),
            jax.ShapeDtypeStruct((3, heads, hidden_rows, head_dim), half),
        ],
        in_specs=[any_spec] * 5,
        out_specs=[vmem_spec] * 2,
        scratch_shapes=[
            pltpu.VMEM((n_ctx, count, width), half),
            pltpu.VMEM((n_ctx, n_dp, depth, 3 * head_dim + LANES), half),
            pltpu.VMEM((3, hidden_all, head_dim), half),
            pltpu.VMEM((3, hidden_all, head_dim), jnp.float32),
            pltpu.VMEM((n_ctx, count, head_dim), half),
            pltpu.VMEM((n_ctx, count, head_dim), half),
            pltpu.VMEM((3, hidden_all, head_dim), half),
            pltpu.VMEM((3, n_ctx, hidden_rows, head_dim), half),
            pltpu.VMEM((n_ctx, n_dp, depth, width), half),
            dma((2, CHUNKS)), dma, dma((2,)),
            dma((n_ctx,)), dma((n_ctx,)), dma((n_ctx,)), dma((n_ctx,)),
            dma((n_dp,)), dma((n_dp,)),
            dma((CHUNKS, lines)), dma((CHUNKS, lines)), dma((CHUNKS, lines)),
            dma((CHUNKS, lines)), dma((CHUNKS, lines)),
            dma((n_ctx,)), dma((n_ctx,)), dma((3, n_ctx)), dma((3, n_ctx)),
            dma, dma((lines,)), dma((lines,)), dma((lines,)), dma((lines,)), dma((lines,)),
            dma((n_dp,)), dma((n_dp,)),
        ],
        compiler_params=pltpu.CompilerParams(
            collective_id=0, has_side_effects=True, vmem_limit_bytes=VMEM_BYTES
        ),
        cost_estimate=pl.CostEstimate(
            flops=flops, bytes_accessed=tokens * width * 2, transcendentals=4 * tokens * hidden_all
        ),
    )(fresh_input, carried, columns, fast_rows, out_weight)

    stepped = previous - update_scale * update.astype(jnp.float32)
    rescale = jnp.sqrt(jnp.mean(previous * previous, axis=-1, keepdims=True) + 1e-06) * lax.rsqrt(
        jnp.mean(stepped * stepped, axis=-1, keepdims=True) + 1e-06
    )
    new_state = (stepped * rescale)[None, None]
    return (passed[None, None], new_state)


def solution(mesh):
    in_specs = (
        P("dp", "ctx", None),
        P("sec", "dp", "ctx", None),
        P("sec", ("ctx", "dp"), None),
        P("sec", ("ctx", "dp"), None),
        P("sec", ("ctx", "dp"), None),
        P("sec", "dp", None, None, "ctx", None),
    )
    out_specs = (P("sec", "dp", "ctx", None), P("sec", "dp", None, None, "ctx", None))
    return jax.shard_map(local, mesh=mesh, in_specs=in_specs, out_specs=out_specs, check_vma=False)
```
